512 devices in a mesh: dp: 16 (over z, core), tensor: 32 (over x, y).
Axes of the slice: x: 4, y: 8, z: 8, core: 2. Of those that a mesh axis runs over, the one named last changes fastest.
Arguments:
- activations: bfloat16 [12288, 4096], P('dp', 'tensor'), may hold values from -6 to 6
- out_grads_t: bfloat16 [5504, 12288], P('tensor', 'dp'), may hold values from -6 to 6
- in_basis: bfloat16 [4096, 4096], P(None, 'tensor'), may hold values from -0.09375 to 0.09375
- out_basis_t: bfloat16 [5504, 5504], P('tensor'), may hold values from -0.078125 to 0.078125
- query_proj: bfloat16 [4, 5504, 4096], P(None, 'tensor', 'dp'), may hold values from -6 to 6
- eigvals: float32 [5504, 4096], P('tensor', 'dp'), may hold values from 0.05 to 5
- damping: float32 [1], replicated, may hold values from 0.05 to 0.2
- lengths: int32 [96], P('dp'), may hold values from 1 to 128, 7680 in all
Outputs:
- scores: float32 [96, 4], P('dp')
The draws below stay inside these ranges and needn't reach their ends.
Inputs may be any that keep to these rules, and one draw needn't show every extreme that they name: `lengths`: the largest token count is exactly 128.
All inputs are finite; a program needn't handle non-finite values. No bound on the sum of `lengths` on one device may be relied on, other than what follows from the above.
Results may differ from the reference program's by a relative error of at most 0.006.
Values may be sent and summed in bfloat16 or wider, within the bound.
No kernel may reach another device: no remote copies, remote signals or barrier semaphores. Data moves between devices by JAX's collectives and lax.ppermute only.
A program may use at most 128 MiB of HBM per device.

```python
import math
import jax
import jax.numpy as jnp
import numpy as np
from jax import lax

D = 4096
FF = 5504
QUERIES = 4
SEQ_LEN = 128
SEQS = 96
TOKENS = 12288


def steps_of(rng, shape, shards, least, top_value):
    def one(dim, parts):
        heights = jax.random.uniform(jax.random.fold_in(jax.random.fold_in(rng, 6), dim), (parts,), jnp.float32, least / len(shards), top_value / len(shards))
        return jnp.repeat(jnp.exp(heights), shape[dim] // parts).reshape((-1,) + (1,) * (len(shape) - dim - 1))

    factor_of = one(*shards[0])
    for cut in shards[1:]:
        factor_of = factor_of * one(*cut)
    return factor_of


def split_up(count, total, limit, lean):
    loads = [(1 << 20) // math.isqrt(standing ** lean) + 1 for standing in range(2, count + 1)]
    spare, counts = total - limit - (count - 1), [1] * (count - 1)
    while spare > 0:
        candidates = [i for i in range(count - 1) if counts[i] < limit]
        mass, budget = sum([loads[i] for i in candidates]), spare
        for i in candidates:
            more = min(limit - counts[i], max(1, budget * loads[i] // mass), spare)
            counts[i] = counts[i] + more
            spare = spare - more
    return np.array([limit] + counts)


def ragged_sizes(rng, count, total, limit, slope):
    if count == 2:
        one = jax.random.randint(rng, (), max(1, total - limit), min(limit, total - 1) + 1)
        return jnp.stack([one, total - one])
    sizes = jnp.asarray(split_up(count, total, limit, slope), jnp.int32)
    twos = (count - 1) // 2
    donor, taker = sizes[1:1 + 2 * twos:2], sizes[2:2 + 2 * twos:2]
    slack = jnp.minimum(donor - 1, limit - taker)
    passed = jax.random.randint(jax.random.fold_in(rng, 1), (twos,), 0, 1 << 20) % (slack + 1)
    sizes = sizes.at[1:1 + 2 * twos:2].set(donor - passed).at[2:2 + 2 * twos:2].set(taker + passed)
    return sizes[jax.random.permutation(jax.random.fold_in(rng, 2), count)]


def gaussian(own_key, dims, deviation, bound, shards=(), kind=jnp.bfloat16):
    values = deviation * jax.random.normal(own_key, dims, jnp.float32)
    if shards:
        values = values * steps_of(own_key, dims, shards, -0.22, 0.18)
    return jnp.clip(values, -bound, bound).astype(kind)


def setup_inputs(seed: int = 0) -> dict:
    streams_of = jax.random.split(jax.random.key(seed), 9)
    return {
        "activations": gaussian(streams_of[0], (TOKENS, D), 1.0, 6.0, ((0, 16), (1, 32))),
        "out_grads_t": gaussian(streams_of[1], (FF, TOKENS), 1.0, 6.0, ((0, 32), (1, 16))),
        "in_basis": gaussian(streams_of[2], (D, D), D ** -0.5, 0.09375, ((1, 32),)),
        "out_basis_t": gaussian(streams_of[3], (FF, FF), FF ** -0.5, 0.078125, ((0, 32),)),
        "query_proj": gaussian(streams_of[4], (QUERIES, FF, D), 1.0, 6.0, ((1, 32), (2, 16))),
        "eigvals": jnp.clip(jnp.exp(math.log(5.0) - 4.6051702 * jax.random.uniform(streams_of[5], (FF, D), jnp.float32) ** steps_of(streams_of[5], (FF, D), ((0, 32), (1, 16)), -0.2, 0.2)), 0.05, 5.0),
        "damping": jnp.clip(jax.random.uniform(streams_of[6], (1,), jnp.float32, 0.05, 0.2), 0.05, 0.2),
        "lengths": ragged_sizes(streams_of[7], SEQS, SEQS * SEQ_LEN * 5 // 8, SEQ_LEN, 1).astype(jnp.int32),
    }


def reference(activations, out_grads_t, in_basis, out_basis_t, query_proj, eigvals, damping, lengths):
    act_proj = jnp.dot(activations, in_basis, preferred_element_type=jnp.float32).astype(jnp.bfloat16)
    grad_full = jnp.dot(out_basis_t, out_grads_t, preferred_element_type=jnp.float32)
    position = lax.broadcasted_iota(jnp.int32, (SEQS, SEQ_LEN), 1)
    keep = (position < lengths[:, None]).astype(jnp.float32).reshape(1, SEQS * SEQ_LEN)
    grad_proj = (grad_full * keep).astype(jnp.bfloat16)
    scaled = (query_proj.astype(jnp.float32) / (eigvals + damping[0])).astype(jnp.bfloat16)
    scaled_wide = scaled.astype(jnp.float32)

    def one_sequence(index):
        start = (index * SEQ_LEN).astype(jnp.int32)
        grad_cols = lax.dynamic_slice_in_dim(grad_proj, start, SEQ_LEN, 1)
        act_rows = lax.dynamic_slice_in_dim(act_proj, start, SEQ_LEN, 0)
        projected = jnp.dot(grad_cols, act_rows, preferred_element_type=jnp.float32)
        return jnp.einsum("ij,qij->q", projected, scaled_wide)

    totals = lax.map(one_sequence, jnp.arange(SEQS, dtype=jnp.int32))
    return totals * ((D * FF * SEQ_LEN) ** -0.5)
```

```python
import jax
import jax.numpy as jnp
from jax import lax
from jax.experimental import pallas as pl
from jax.experimental.pallas import tpu as pltpu
from jax.sharding import PartitionSpec as P

NX, NY, NZ = 4, 8, 8
XG = [[x * NY + y for x in range(NX)] for y in range(NY)]
YG = [[x * NY + y for y in range(NY)] for x in range(NX)]
ZG = [[z * 2 + c for z in range(NZ)] for c in range(2)]
CG = [[z * 2 + c for c in range(2)] for z in range(NZ)]
SEQ = 128
PAD = 176


def score_kernel(g_ref, a_ref, s_ref, o_ref, p_ref):
    seqs = g_ref.shape[2] // SEQ
    queries = s_ref.shape[1] // 2

    def block(step, _):
        fx = step // 4
        pair = lax.rem(step, 4)
        high = pair // 2
        core = lax.rem(pair, 2)
        for s in range(seqs):
            tokens = pl.ds(s * SEQ, SEQ)
            rhs = jnp.concatenate([a_ref[2 * pair, tokens, :], a_ref[2 * pair + 1, tokens, :]], axis=1)
            p_ref[s] = jnp.dot(g_ref[fx, :, tokens], rhs, preferred_element_type=jnp.float32)
        for half in range(2):
            lanes = pl.ds(half * 128, 128)
            slots = [lax.rem(2 * q + half - 2 * fx - high + 8, 8) for q in range(queries)]

            def rows(r, acc):
                sl = pl.ds(pl.multiple_of(r * 16, 16), 16)
                w = [s_ref[core, 2 * q + half, slots[q], sl, :].astype(jnp.float32) for q in range(queries)]
                out = []
                for s in range(seqs):
                    p = p_ref[s, sl, lanes]
                    for q in range(queries):
                        t = p * w[q]
                        out.append(acc[s * queries + q] + t[:8] + t[8:])
                return tuple(out)

            zero = tuple(jnp.zeros((8, 128), jnp.float32) for _ in range(seqs * queries))
            acc = lax.fori_loop(0, PAD // 16, rows, zero)
            for n in range(seqs * queries):
                o_ref[n] += acc[n]
        return 0

    o_ref[...] = jnp.zeros_like(o_ref)
    lax.fori_loop(0, 16, block, 0)


def score_tiles(g4, a8, s2):
    seqs = g4.shape[2] // SEQ
    queries = s2.shape[1] // 2
    return pl.pallas_call(
        score_kernel,
        out_shape=jax.ShapeDtypeStruct((seqs * queries, 8, 128), jnp.float32),
        in_specs=[pl.BlockSpec(memory_space=pltpu.VMEM)] * 3,
        out_specs=pl.BlockSpec(memory_space=pltpu.VMEM),
        scratch_shapes=[pltpu.VMEM((seqs, PAD, 256), jnp.float32)],
        compiler_params=pltpu.CompilerParams(vmem_limit_bytes=40 * 1024 * 1024),
        cost_estimate=pl.CostEstimate(flops=2 * 768 * 704 * 1024, bytes_accessed=9_000_000, transcendentals=0),
    )(g4, a8, s2)


def add_parts(parts):
    wide = [parts[n].astype(jnp.float32) for n in range(NX)]
    return (wide[0] + wide[1]) + (wide[2] + wide[3])


def local(activations, out_grads_t, in_basis, out_basis_t, query_proj, eigvals, damping, lengths):
    bf, f32 = jnp.bfloat16, jnp.float32
    tokens, width = activations.shape[0], out_grads_t.shape[0]
    seqs, queries = lengths.shape[0], query_proj.shape[0]
    seq_len = tokens // seqs
    kx = lax.shift_right_logical(lax.axis_index("tensor"), 3)
    kz = lax.shift_right_logical(lax.axis_index("dp"), 1)
    base = 2 * kx + (kz & 1)

    y8 = lax.all_gather(out_grads_t, "tensor", axis_index_groups=YG)
    x8 = lax.all_gather(activations, "tensor", axis_index_groups=YG)

    scaled = (query_proj.astype(f32) / (eigvals + damping[0])).astype(bf)
    scaled = jnp.pad(scaled, ((0, 0), (0, PAD - width), (0, 0)))
    pieces = scaled.reshape(queries, PAD, 2, 128).transpose(0, 2, 1, 3).reshape(8, PAD, 128)
    got = []
    for r in range(8):
        perm = []
        for z in range(NZ):
            for c in range(2):
                for x in range(NX):
                    for y in range(NY):
                        zz = (2 * x + z % 2 + r) % 8
                        perm.append(((z * 2 + c) * 32 + x * NY + y, (zz * 2 + c) * 32 + (z // 2) * NY + y))
        piece = lax.dynamic_index_in_dim(pieces, (base + r) & 7, 0, keepdims=False)
        got.append(lax.ppermute(piece, ("dp", "tensor"), perm))
    s8 = lax.all_gather(jnp.stack(got), "dp", axis_index_groups=ZG)
    s2 = lax.all_gather(s8, "dp", axis_index_groups=CG)

    v4 = out_basis_t.reshape(width, NX, NY * width).transpose(1, 0, 2)
    v4 = lax.all_to_all(v4, "tensor", 0, 0, axis_index_groups=XG)
    u4 = lax.all_to_all(in_basis.reshape(NX, NY * 128, 128), "tensor", 0, 0, axis_index_groups=XG)

    g_part = jnp.einsum("xjk,kt->xjt", v4, y8.reshape(NY * width, tokens), preferred_element_type=f32).astype(bf)
    g_parts = lax.all_to_all(g_part, "tensor", 0, 0, axis_index_groups=XG)
    position = lax.broadcasted_iota(jnp.int32, (seqs, seq_len), 1)
    keep = (position < lengths[:, None]).astype(f32).reshape(1, tokens)
    g = (add_parts(g_parts) * keep).astype(bf)
    g4 = lax.all_gather(jnp.pad(g, ((0, PAD - width), (0, 0))), "tensor", axis_index_groups=XG)

    a_part = jnp.einsum("yte,xyed->xtd", x8, u4.reshape(NX, NY, 128, 128), preferred_element_type=f32).astype(bf)
    a_parts = lax.all_to_all(a_part, "tensor", 0, 0, axis_index_groups=XG)
    a = add_parts(a_parts).astype(bf)
    a8 = lax.all_gather(a, "tensor", axis_index_groups=YG)

    part = score_tiles(g4, a8, s2).sum((1, 2))
    tile = jnp.broadcast_to(jnp.pad(part, (0, 128 - part.shape[0])), (NX * NY, 8, 128))
    totals = lax.all_to_all(tile, "tensor", 0, 0)[:, 0, : part.shape[0]].sum(0)
    norm_factor = (in_basis.shape[0] * out_basis_t.shape[1] * seq_len) ** (-0.5)
    return totals.reshape(seqs, queries) * norm_factor


def solution(mesh):
    placed = (
        P("dp", "tensor"),
        P("tensor", "dp"),
        P(None, "tensor"),
        P("tensor", None),
        P(None, "tensor", "dp"),
        P("tensor", "dp"),
        P(),
        P("dp"),
    )
    return jax.shard_map(
        local, mesh=mesh, in_specs=placed, out_specs=P("dp", None), check_vma=False
    )
```

```python
import jax
import jax.numpy as jnp
from jax import lax
from jax.experimental import pallas as pl
from jax.experimental.pallas import tpu as pltpu
from jax.sharding import PartitionSpec as P

NX, NY, NZ = 4, 8, 8
XG = [[x * NY + y for x in range(NX)] for y in range(NY)]
YG = [[x * NY + y for y in range(NY)] for x in range(NX)]
ZG = [[z * 2 + c for z in range(NZ)] for c in range(2)]
SEQ = 128
PAD = 176


def shift_x(array, by):
    perm = [(x * NY + y, (x + by) % NX * NY + y) for x in range(NX) for y in range(NY)]
    return lax.ppermute(array, "tensor", perm)


def score_kernel(where_ref, g0_ref, g1_ref, g2_ref, g3_ref, a_ref, own_ref, other_ref, o_ref, at_ref, sum_ref):
    core, kx = where_ref[0], where_ref[1]
    tokens = g0_ref.shape[1]
    queries = own_ref.shape[0] // 2
    row = 0
    for high in range(2):
        for c in (core, 1 - core):
            for half in range(2):
                at_ref[pl.ds(row, 128), :] = a_ref[4 * high + 2 * c + half]
                row += 128
    sum_ref[...] = jnp.zeros_like(sum_ref)
    for d, g_ref in enumerate((g0_ref, g1_ref, g2_ref, g3_ref)):
        fx = (kx - d) & (NX - 1)

        def one(q, _):
            tiles = []
            for high in range(2):
                for s_ref in (own_ref, other_ref):
                    for half in range(2):
                        p = 2 * q + half
                        tiles.append(s_ref[p, (p - 2 * fx - high) & 7])
            lhs = jnp.concatenate(tiles, axis=1)
            t = jnp.dot(lhs, at_ref[...], preferred_element_type=jnp.float32)
            t = t * g_ref[...].astype(jnp.float32)
            sum_ref[q] += t.reshape(PAD // 8, 8, tokens).sum(0)
            return 0

        lax.fori_loop(0, queries, one, 0)
    lane = lax.broadcasted_iota(jnp.int32, (1, 128), 1)
    out = jnp.zeros((1, 128), jnp.float32)
    for q in range(queries):
        per_token = jnp.sum(sum_ref[q], axis=0, keepdims=True)
        for s in range(tokens // SEQ):
            value = jnp.sum(per_token[:, s * SEQ : (s + 1) * SEQ], axis=1, keepdims=True)
            out = jnp.where(lane == s * queries + q, value, out)
    o_ref[...] = jnp.broadcast_to(out, o_ref.shape)


def score_tiles(where, gs, at, own, other):
    tokens = at.shape[2]
    queries = own.shape[0] // 2
    return pl.pallas_call(
        score_kernel,
        out_shape=jax.ShapeDtypeStruct((NX * NY, 128), jnp.float32),
        in_specs=[pl.BlockSpec(memory_space=pltpu.SMEM)] + [pl.BlockSpec(memory_space=pltpu.VMEM)] * 7,
        out_specs=pl.BlockSpec(memory_space=pltpu.VMEM),
        scratch_shapes=[
            pltpu.VMEM((NY * 128, tokens), jnp.bfloat16),
            pltpu.VMEM((queries, 8, tokens), jnp.float32),
        ],
        compiler_params=pltpu.CompilerParams(vmem_limit_bytes=40 * 1024 * 1024),
        cost_estimate=pl.CostEstimate(
            flops=2 * NX * queries * PAD * NY * 128 * tokens, bytes_accessed=9_000_000, transcendentals=0
        ),
    )(where, *gs, at, own, other)


def add_parts(parts):
    wide = [parts[n].astype(jnp.float32) for n in range(NX)]
    return (wide[0] + wide[1]) + (wide[2] + wide[3])


def local(activations, out_grads_t, in_basis, out_basis_t, query_proj, eigvals, damping, lengths):
    bf, f32 = jnp.bfloat16, jnp.float32
    tokens, width = activations.shape[0], out_grads_t.shape[0]
    seqs, queries = lengths.shape[0], query_proj.shape[0]
    seq_len = tokens // seqs
    kx = lax.shift_right_logical(lax.axis_index("tensor"), 3)
    dp = lax.axis_index("dp")
    base = 2 * kx + (lax.shift_right_logical(dp, 1) & 1)

    grads = jnp.pad(out_grads_t.reshape(width, seqs, seq_len).transpose(1, 0, 2), ((0, 0), (0, PAD - width), (0, 0)))
    both = jnp.concatenate([activations, grads.reshape(seqs * PAD, seq_len)], axis=0)
    both = lax.all_gather(both, "tensor", axis_index_groups=YG)
    x8 = both[:, :tokens]
    y8 = both[:, tokens:].reshape(NY, seqs, PAD, seq_len)[:, :, :width]

    scaled = (query_proj.astype(f32) / (eigvals + damping[0])).astype(bf)
    scaled = jnp.pad(scaled, ((0, 0), (0, PAD - width), (0, 0)))
    pieces = scaled.reshape(queries, PAD, 2, 128).transpose(0, 2, 1, 3).reshape(8, PAD, 128)
    got = []
    for r in range(8):
        perm = []
        for z in range(NZ):
            for c in range(2):
                for x in range(NX):
                    for y in range(NY):
                        zz = (2 * x + z % 2 + r) % 8
                        perm.append(((z * 2 + c) * 32 + x * NY + y, (zz * 2 + c) * 32 + (z // 2) * NY + y))
        piece = lax.dynamic_index_in_dim(pieces, (base + r) & 7, 0, keepdims=False)
        got.append(lax.ppermute(piece, ("dp", "tensor"), perm))
    own = lax.all_gather(jnp.stack(got), "dp", axis_index_groups=ZG)
    other = lax.ppermute(own, "dp", [(n, n ^ 1) for n in range(16)])

    v4 = out_basis_t.reshape(width, NX, NY * width).transpose(1, 0, 2)
    v4 = lax.all_to_all(v4, "tensor", 0, 0, axis_index_groups=XG)
    u4 = lax.all_to_all(in_basis.reshape(NX, NY * 128, 128), "tensor", 0, 0, axis_index_groups=XG)

    a_part = jnp.einsum("xyed,yte->xdt", u4.reshape(NX, NY, 128, 128), x8, preferred_element_type=f32).astype(bf)
    a_parts = lax.all_to_all(a_part, "tensor", 0, 0, axis_index_groups=XG)
    at = lax.all_gather(add_parts(a_parts).astype(bf), "tensor", axis_index_groups=YG)

    y8 = y8.transpose(0, 2, 1, 3).reshape(NY * width, tokens)
    g_part = jnp.einsum("xjk,kt->xjt", v4, y8, preferred_element_type=f32).astype(bf)
    g_parts = lax.all_to_all(g_part, "tensor", 0, 0, axis_index_groups=XG)
    position = lax.broadcasted_iota(jnp.int32, (seqs, seq_len), 1)
    keep = (position < lengths[:, None]).astype(f32).reshape(1, tokens)
    g = (add_parts(g_parts) * keep).astype(bf)
    g = jnp.pad(g, ((0, PAD - width), (0, 0)))
    gs = [g] + [shift_x(g, d) for d in range(1, NX)]

    where = jnp.stack([dp & 1, kx]).astype(jnp.int32)
    tile = score_tiles(where, gs, at, own, other)
    totals = lax.all_to_all(tile, "tensor", 0, 0, tiled=True).sum(0)[: seqs * queries]
    norm_factor = (in_basis.shape[0] * out_basis_t.shape[1] * seq_len) ** (-0.5)
    return totals.reshape(seqs, queries) * norm_factor


def solution(mesh):
    placed = (
        P("dp", "tensor"),
        P("tensor", "dp"),
        P(None, "tensor"),
        P("tensor", None),
        P(None, "tensor", "dp"),
        P("tensor", "dp"),
        P(),
        P("dp"),
    )
    return jax.shard_map(
        local, mesh=mesh, in_specs=placed, out_specs=P("dp", None), check_vma=False
    )
```

```python
import jax
import jax.numpy as jnp
from jax import lax
from jax.experimental import pallas as pl
from jax.experimental.pallas import tpu as pltpu
from jax.sharding import PartitionSpec as P

NX, NY, NZ = 4, 8, 8
XG = [[x * NY + y for x in range(NX)] for y in range(NY)]
YG = [[x * NY + y for y in range(NY)] for x in range(NX)]
ZG = [[z * 2 + c for z in range(NZ)] for c in range(2)]
SEQ = 128
PAD = 176


def shift_x(array, by):
    perm = [(x * NY + y, (x + by) % NX * NY + y) for x in range(NX) for y in range(NY)]
    return lax.ppermute(array, "tensor", perm)


def score_kernel(kx_ref, g0_ref, g1_ref, g2_ref, g3_ref, a_ref, s_ref, o_ref):
    q = pl.program_id(0)
    queries = pl.num_programs(0)
    tokens = g0_ref.shape[1]
    acc = jnp.zeros((8, tokens), jnp.float32)
    for d, g_ref in enumerate((g0_ref, g1_ref, g2_ref, g3_ref)):
        fx = (kx_ref[0] - d) & (NX - 1)
        tiles = [s_ref[half, core, fx, high] for high in range(2) for core in range(2) for half in range(2)]
        t = jnp.dot(jnp.concatenate(tiles, axis=1), a_ref[...], preferred_element_type=jnp.float32)
        acc += (t * g_ref[...].astype(jnp.float32)).reshape(PAD // 8, 8, tokens).sum(0)
    per_token = jnp.sum(acc, axis=0, keepdims=True)
    lane = lax.broadcasted_iota(jnp.int32, o_ref.shape, 1)

    @pl.when(q == 0)
    def _():
        o_ref[...] = jnp.zeros_like(o_ref)

    out = o_ref[...]
    for s in range(tokens // SEQ):
        value = jnp.sum(per_token[:, s * SEQ : (s + 1) * SEQ], axis=1, keepdims=True)
        out = jnp.where(lane == s * queries + q, value, out)
    o_ref[...] = out


def score_tiles(kx, gs, at, tiles):
    tokens = at.shape[1]
    queries = tiles.shape[0] // 2
    whole = lambda q: (0, 0)
    return pl.pallas_call(
        score_kernel,
        grid=(queries,),
        out_shape=jax.ShapeDtypeStruct((NX * NY, 128), jnp.float32),
        in_specs=[pl.BlockSpec(memory_space=pltpu.SMEM)]
        + [pl.BlockSpec((PAD, tokens), whole)] * NX
        + [pl.BlockSpec(at.shape, whole), pl.BlockSpec((2,) + tiles.shape[1:], lambda q: (q, 0, 0, 0, 0, 0))],
        out_specs=pl.BlockSpec((NX * NY, 128), whole),
        compiler_params=pltpu.CompilerParams(vmem_limit_bytes=48 * 1024 * 1024),
        cost_estimate=pl.CostEstimate(
            flops=2 * NX * queries * PAD * NY * 128 * tokens, bytes_accessed=9_000_000, transcendentals=0
        ),
    )(kx, *gs, at, tiles)


def add_parts(parts):
    wide = [parts[n].astype(jnp.float32) for n in range(NX)]
    return (wide[0] + wide[1]) + (wide[2] + wide[3])


def local(activations, out_grads_t, in_basis, out_basis_t, query_proj, eigvals, damping, lengths):
    bf, f32 = jnp.bfloat16, jnp.float32
    tokens, width = activations.shape[0], out_grads_t.shape[0]
    seqs, queries = lengths.shape[0], query_proj.shape[0]
    seq_len = tokens // seqs
    kx = lax.shift_right_logical(lax.axis_index("tensor"), 3)

    grads = jnp.pad(out_grads_t.reshape(width, seqs, seq_len).transpose(1, 0, 2), ((0, 0), (0, PAD - width), (0, 0)))
    both = jnp.concatenate([activations, grads.reshape(seqs * PAD, seq_len)], axis=0)
    both = lax.all_gather(both, "tensor", axis_index_groups=YG)
    x8 = both[:, :tokens]
    y8 = both[:, tokens:].reshape(NY, seqs, PAD, seq_len)[:, :, :width]

    scaled = (query_proj.astype(f32) / (eigvals + damping[0])).astype(bf)
    scaled = jnp.pad(scaled, ((0, 0), (0, PAD - width), (0, 0)))
    pieces = scaled.reshape(queries, PAD, 2, 128).transpose(0, 2, 1, 3).reshape(8, PAD, 128)
    pieces = lax.all_to_all(pieces, "dp", 0, 0, axis_index_groups=ZG)
    pieces = lax.all_to_all(pieces.reshape(NX, 2, PAD, 128), "tensor", 0, 0, axis_index_groups=XG)
    tiles = lax.all_gather(pieces, "dp").reshape(NZ, 2, NX, 2, PAD, 128)

    v4 = out_basis_t.reshape(width, NX, NY * width).transpose(1, 0, 2)
    vs = [lax.dynamic_index_in_dim(v4, (kx + d) & (NX - 1), 0, keepdims=False) for d in range(NX)]
    vs = [vs[0]] + [shift_x(vs[d], d) for d in range(1, NX)]
    u4 = lax.all_to_all(in_basis.reshape(NX, NY * 128, 128), "tensor", 0, 0, axis_index_groups=XG)

    tie = (vs[1][:1, :1] + vs[2][:1, :1] + vs[3][:1, :1]) * 0
    u4 = lax.dynamic_update_slice(u4, u4[:1, :1, :1] + tie[None], (0, 0, 0))
    a_part = jnp.einsum("xyed,yte->xdt", u4.reshape(NX, NY, 128, 128), x8, preferred_element_type=f32).astype(bf)
    a_parts = lax.all_to_all(a_part, "tensor", 0, 0, axis_index_groups=XG)
    at = jnp.broadcast_to(add_parts(a_parts).astype(bf), (NY, 128, tokens))
    at = lax.all_to_all(at, "tensor", 0, 0, axis_index_groups=YG)

    y8 = y8.transpose(0, 2, 1, 3).reshape(NY * width, tokens)
    g_parts = [jnp.dot(v, y8, preferred_element_type=f32).astype(bf) for v in vs]
    g_parts = [g_parts[0]] + [shift_x(g_parts[d], -d) for d in range(1, NX)]
    position = lax.broadcasted_iota(jnp.int32, (seqs, seq_len), 1)
    keep = (position < lengths[:, None]).astype(f32).reshape(1, tokens)
    g = (add_parts(g_parts) * keep).astype(bf)
    g = jnp.pad(g, ((0, PAD - width), (0, 0)))
    gs = [g] + [shift_x(g, d) for d in range(1, NX)]

    tile = score_tiles(kx.reshape(1), gs, at.reshape(NY * 128, tokens), tiles)
    totals = lax.all_to_all(tile, "tensor", 0, 0, tiled=True).sum(0)[: seqs * queries]
    norm_factor = (in_basis.shape[0] * out_basis_t.shape[1] * seq_len) ** (-0.5)
    return totals.reshape(seqs, queries) * norm_factor


def solution(mesh):
    placed = (
        P("dp", "tensor"),
        P("tensor", "dp"),
        P(None, "tensor"),
        P("tensor", None),
        P(None, "tensor", "dp"),
        P("tensor", "dp"),
        P(),
        P("dp"),
    )
    return jax.shard_map(
        local, mesh=mesh, in_specs=placed, out_specs=P("dp", None), check_vma=False
    )
```

```python
import jax
import jax.numpy as jnp
from jax import lax
from jax.experimental import pallas as pl
from jax.experimental.pallas import tpu as pltpu
from jax.sharding import PartitionSpec as P

NX, NY, NZ = 4, 8, 8
XG = [[x * NY + y for x in range(NX)] for y in range(NY)]
YG = [[x * NY + y for y in range(NY)] for x in range(NX)]
ZG = [[z * 2 + c for z in range(NZ)] for c in range(2)]
SEQ = 128
PAD = 176


def shift_x(array, by):
    perm = [(x * NY + y, (x + by) % NX * NY + y) for x in range(NX) for y in range(NY)]
    return lax.ppermute(array, "tensor", perm)


def columns_kernel(kx_ref, v_ref, o0_ref, o1_ref, o2_ref, o3_ref, all_ref):
    rows, columns = v_ref.shape
    width = columns // (NX * NY)
    for x in range(NX):
        for y in range(NY):
            first = (x * NY + y) * width
            if first + PAD <= columns:
                block = v_ref[:, first : first + PAD]
            else:
                block = jnp.concatenate(
                    [v_ref[:, first:], jnp.zeros((rows, first + PAD - columns), v_ref.dtype)], axis=1
                )
            all_ref[x, :, y * PAD : (y + 1) * PAD] = block
    for d, o_ref in enumerate((o0_ref, o1_ref, o2_ref, o3_ref)):
        o_ref[...] = all_ref[(kx_ref[0] + d) & (NX - 1)]


def column_blocks(kx, v):
    one = jax.ShapeDtypeStruct((v.shape[0], NY * PAD), v.dtype)
    vmem = pl.BlockSpec(memory_space=pltpu.VMEM)
    return pl.pallas_call(
        columns_kernel,
        out_shape=[one] * NX,
        in_specs=[pl.BlockSpec(memory_space=pltpu.SMEM), vmem],
        out_specs=[vmem] * NX,
        scratch_shapes=[pltpu.VMEM((NX,) + one.shape, v.dtype)],
        compiler_params=pltpu.CompilerParams(vmem_limit_bytes=24 * 1024 * 1024),
        cost_estimate=pl.CostEstimate(flops=0, bytes_accessed=4_000_000, transcendentals=0),
    )(kx, v)


def score_kernel(kx_ref, g0_ref, g1_ref, g2_ref, g3_ref, a_ref, s_ref, o_ref):
    q = pl.program_id(0)
    queries = pl.num_programs(0)
    tokens = g0_ref.shape[1]
    acc = jnp.zeros((8, tokens), jnp.float32)
    for d, g_ref in enumerate((g0_ref, g1_ref, g2_ref, g3_ref)):
        fx = (kx_ref[0] - d) & (NX - 1)
        tiles = [s_ref[half, core, fx, high] for high in range(2) for core in range(2) for half in range(2)]
        t = jnp.dot(jnp.concatenate(tiles, axis=1), a_ref[...], preferred_element_type=jnp.float32)
        acc += (t * g_ref[...].astype(jnp.float32)).reshape(PAD // 8, 8, tokens).sum(0)
    per_token = jnp.sum(acc, axis=0, keepdims=True)
    lane = lax.broadcasted_iota(jnp.int32, o_ref.shape, 1)

    @pl.when(q == 0)
    def _():
        o_ref[...] = jnp.zeros_like(o_ref)

    out = o_ref[...]
    for s in range(tokens // SEQ):
        value = jnp.sum(per_token[:, s * SEQ : (s + 1) * SEQ], axis=1, keepdims=True)
        out = jnp.where(lane == s * queries + q, value, out)
    o_ref[...] = out


def score_tiles(kx, gs, at, tiles):
    tokens = at.shape[1]
    queries = tiles.shape[0] // 2
    whole = lambda q: (0, 0)
    return pl.pallas_call(
        score_kernel,
        grid=(queries,),
        out_shape=jax.ShapeDtypeStruct((NX * NY, 128), jnp.float32),
        in_specs=[pl.BlockSpec(memory_space=pltpu.SMEM)]
        + [pl.BlockSpec((PAD, tokens), whole)] * NX
        + [pl.BlockSpec(at.shape, whole), pl.BlockSpec((2,) + tiles.shape[1:], lambda q: (q, 0, 0, 0, 0, 0))],
        out_specs=pl.BlockSpec((NX * NY, 128), whole),
        compiler_params=pltpu.CompilerParams(vmem_limit_bytes=48 * 1024 * 1024),
        cost_estimate=pl.CostEstimate(
            flops=2 * NX * queries * PAD * NY * 128 * tokens, bytes_accessed=9_000_000, transcendentals=0
        ),
    )(kx, *gs, at, tiles)


def add_parts(parts):
    wide = [parts[n].astype(jnp.float32) for n in range(NX)]
    return (wide[0] + wide[1]) + (wide[2] + wide[3])


def local(activations, out_grads_t, in_basis, out_basis_t, query_proj, eigvals, damping, lengths):
    bf, f32 = jnp.bfloat16, jnp.float32
    tokens, width = activations.shape[0], out_grads_t.shape[0]
    seqs, queries = lengths.shape[0], query_proj.shape[0]
    seq_len = tokens // seqs
    kx = lax.shift_right_logical(lax.axis_index("tensor"), 3)

    grads = jnp.pad(out_grads_t.reshape(width, seqs, seq_len).transpose(1, 0, 2), ((0, 0), (0, PAD - width), (0, 0)))
    both = jnp.concatenate([activations, grads.reshape(seqs * PAD, seq_len)], axis=0)
    both = lax.all_gather(both, "tensor", axis_index_groups=YG)
    x8 = both[:, :tokens]
    y8 = both[:, tokens:].reshape(NY, seqs, PAD, seq_len)

    scaled = (query_proj.astype(f32) / (eigvals + damping[0])).astype(bf)
    scaled = jnp.pad(scaled, ((0, 0), (0, PAD - width), (0, 0)))
    pieces = scaled.reshape(queries, PAD, 2, 128).transpose(0, 2, 1, 3).reshape(8, PAD, 128)
    blocks = column_blocks(kx.reshape(1), out_basis_t)
    vs = [blocks[0]] + [shift_x(blocks[d], d) for d in range(1, NX)]
    pieces = lax.all_to_all(pieces, "dp", 0, 0, axis_index_groups=ZG)
    rows = NY * 128
    mixed = jnp.concatenate([in_basis.reshape(NX, rows, 128), pieces.reshape(NX, 2 * PAD, 128)], axis=1)
    tie = (vs[1][:1, :1] + vs[2][:1, :1] + vs[3][:1, :1]) * 0
    mixed = lax.dynamic_update_slice(mixed, mixed[:1, :1, :1] + tie[None], (0, 0, 0))
    mixed = lax.all_to_all(mixed, "tensor", 0, 0, axis_index_groups=XG)
    u4 = mixed[:, :rows]
    pieces = mixed[:, rows:].reshape(NX, 2, PAD, 128)
    tiles = lax.all_gather(pieces, "dp").reshape(NZ, 2, NX, 2, PAD, 128)

    a_part = jnp.einsum("xyed,yte->xdt", u4.reshape(NX, NY, 128, 128), x8, preferred_element_type=f32).astype(bf)
    a_parts = lax.all_to_all(a_part, "tensor", 0, 0, axis_index_groups=XG)
    at = jnp.broadcast_to(add_parts(a_parts).astype(bf), (NY, 128, tokens))
    at = lax.all_to_all(at, "tensor", 0, 0, axis_index_groups=YG)

    y8 = y8.transpose(0, 2, 1, 3).reshape(NY * PAD, tokens)
    g_parts = [jnp.dot(v, y8, preferred_element_type=f32).astype(bf) for v in vs]
    g_parts = [g_parts[0]] + [shift_x(g_parts[d], -d) for d in range(1, NX)]
    position = lax.broadcasted_iota(jnp.int32, (seqs, seq_len), 1)
    keep = (position < lengths[:, None]).astype(f32).reshape(1, tokens)
    g = (add_parts(g_parts) * keep).astype(bf)
    g = jnp.pad(g, ((0, PAD - width), (0, 0)))
    gs = [g] + [shift_x(g, d) for d in range(1, NX)]

    tile = score_tiles(kx.reshape(1), gs, at.reshape(NY * 128, tokens), tiles)
    totals = lax.all_to_all(tile, "tensor", 0, 0, tiled=True).sum(0)[: seqs * queries]
    norm_factor = (in_basis.shape[0] * out_basis_t.shape[1] * seq_len) ** (-0.5)
    return totals.reshape(seqs, queries) * norm_factor


def solution(mesh):
    placed = (
        P("dp", "tensor"),
        P("tensor", "dp"),
        P(None, "tensor"),
        P("tensor", None),
        P(None, "tensor", "dp"),
        P("tensor", "dp"),
        P(),
        P("dp"),
    )
    return jax.shard_map(
        local, mesh=mesh, in_specs=placed, out_specs=P("dp", None), check_vma=False
    )
```

```python
import jax
import jax.numpy as jnp
from jax import lax
from jax.experimental import pallas as pl
from jax.experimental.pallas import tpu as pltpu
from jax.sharding import PartitionSpec as P

NX, NY, NZ = 4, 8, 8
XG = [[x * NY + y for x in range(NX)] for y in range(NY)]
YG = [[x * NY + y for y in range(NY)] for x in range(NX)]
ZG = [[z * 2 + c for z in range(NZ)] for c in range(2)]
SEQ = 128
PAD = 176


def shift_x(array, by):
    perm = [(x * NY + y, (x + by) % NX * NY + y) for x in range(NX) for y in range(NY)]
    return lax.ppermute(array, "tensor", perm)


def pack_kernel(x_ref, y_ref, o_ref):
    tokens = x_ref.shape[0]
    width = y_ref.shape[0]
    o_ref[:tokens] = x_ref[...]
    for s in range(y_ref.shape[1] // SEQ):
        block = y_ref[:, s * SEQ : (s + 1) * SEQ]
        first = tokens + s * PAD
        o_ref[first : first + PAD] = jnp.concatenate([block, jnp.zeros((PAD - width, SEQ), block.dtype)], axis=0)


def packed(x, y):
    vmem = pl.BlockSpec(memory_space=pltpu.VMEM)
    return pl.pallas_call(
        pack_kernel,
        out_shape=jax.ShapeDtypeStruct((x.shape[0] + y.shape[1] // SEQ * PAD, SEQ), x.dtype),
        in_specs=[vmem] * 2,
        out_specs=vmem,
        cost_estimate=pl.CostEstimate(flops=0, bytes_accessed=1_000_000, transcendentals=0),
    )(x, y)


def columns_kernel(kx_ref, v_ref, o0_ref, o1_ref, o2_ref, o3_ref, all_ref):
    rows, columns = v_ref.shape
    width = columns // (NX * NY)
    for x in range(NX):
        for y in range(NY):
            first = (x * NY + y) * width
            if first + PAD <= columns:
                block = v_ref[:, first : first + PAD]
            else:
                block = jnp.concatenate(
                    [v_ref[:, first:], jnp.zeros((rows, first + PAD - columns), v_ref.dtype)], axis=1
                )
            all_ref[x, :, y * PAD : (y + 1) * PAD] = block
    for d, o_ref in enumerate((o0_ref, o1_ref, o2_ref, o3_ref)):
        o_ref[...] = all_ref[(kx_ref[0] + d) & (NX - 1)]


def column_blocks(kx, v):
    one = jax.ShapeDtypeStruct((v.shape[0], NY * PAD), v.dtype)
    vmem = pl.BlockSpec(memory_space=pltpu.VMEM)
    return pl.pallas_call(
        columns_kernel,
        out_shape=[one] * NX,
        in_specs=[pl.BlockSpec(memory_space=pltpu.SMEM), vmem],
        out_specs=[vmem] * NX,
        scratch_shapes=[pltpu.VMEM((NX,) + one.shape, v.dtype)],
        compiler_params=pltpu.CompilerParams(vmem_limit_bytes=24 * 1024 * 1024),
        cost_estimate=pl.CostEstimate(flops=0, bytes_accessed=4_000_000, transcendentals=0),
    )(kx, v)


def score_kernel(kx_ref, g0_ref, g1_ref, g2_ref, g3_ref, a_ref, s_ref, o_ref, lhs_ref):
    q = pl.program_id(0)
    queries = pl.num_programs(0)
    tokens = g0_ref.shape[1]
    for d in range(NX):
        fx = (kx_ref[0] - d) & (NX - 1)
        for y in range(NY):
            lhs_ref[d * PAD : (d + 1) * PAD, y * 128 : (y + 1) * 128] = s_ref[y % 2, y // 2 % 2, fx, y // 4]
    t = jnp.dot(lhs_ref[...], a_ref[...], preferred_element_type=jnp.float32)
    acc = jnp.zeros((8, tokens), jnp.float32)
    for d, g_ref in enumerate((g0_ref, g1_ref, g2_ref, g3_ref)):
        part = t[d * PAD : (d + 1) * PAD] * g_ref[...].astype(jnp.float32)
        acc += part.reshape(PAD // 8, 8, tokens).sum(0)
    per_token = jnp.sum(acc, axis=0, keepdims=True)
    lane = lax.broadcasted_iota(jnp.int32, o_ref.shape, 1)

    @pl.when(q == 0)
    def _():
        o_ref[...] = jnp.zeros_like(o_ref)

    out = o_ref[...]
    for s in range(tokens // SEQ):
        value = jnp.sum(per_token[:, s * SEQ : (s + 1) * SEQ], axis=1, keepdims=True)
        out = jnp.where(lane == s * queries + q, value, out)
    o_ref[...] = out


def score_tiles(kx, gs, at, tiles):
    tokens = at.shape[1]
    queries = tiles.shape[0] // 2
    whole = lambda q: (0, 0)
    return pl.pallas_call(
        score_kernel,
        grid=(queries,),
        out_shape=jax.ShapeDtypeStruct((NX * NY, 128), jnp.float32),
        in_specs=[pl.BlockSpec(memory_space=pltpu.SMEM)]
        + [pl.BlockSpec((PAD, tokens), whole)] * NX
        + [pl.BlockSpec(at.shape, whole), pl.BlockSpec((2,) + tiles.shape[1:], lambda q: (q, 0, 0, 0, 0, 0))],
        out_specs=pl.BlockSpec((NX * NY, 128), whole),
        scratch_shapes=[pltpu.VMEM((NX * PAD, NY * 128), jnp.bfloat16)],
        compiler_params=pltpu.CompilerParams(vmem_limit_bytes=48 * 1024 * 1024),
        cost_estimate=pl.CostEstimate(
            flops=2 * NX * queries * PAD * NY * 128 * tokens, bytes_accessed=9_000_000, transcendentals=0
        ),
    )(kx, *gs, at, tiles)


def add_parts(parts):
    wide = [parts[n].astype(jnp.float32) for n in range(NX)]
    return (wide[0] + wide[1]) + (wide[2] + wide[3])


def after(array, zero):
    first = (0,) * array.ndim
    corner = lax.slice(array, first, (1,) * array.ndim)
    return lax.dynamic_update_slice(array, corner + zero.reshape(corner.shape), first)


def local(activations, out_grads_t, in_basis, out_basis_t, query_proj, eigvals, damping, lengths):
    bf, f32 = jnp.bfloat16, jnp.float32
    tokens, width = activations.shape[0], out_grads_t.shape[0]
    seqs, queries = lengths.shape[0], query_proj.shape[0]
    seq_len = tokens // seqs
    kx = lax.shift_right_logical(lax.axis_index("tensor"), 3)

    both = packed(activations, out_grads_t)
    both = lax.all_gather(both, "tensor", axis_index_groups=YG)
    x8 = both[:, :tokens]
    y8 = both[:, tokens:].reshape(NY, seqs, PAD, seq_len)

    scaled = (query_proj.astype(f32) / (eigvals + damping[0])).astype(bf)
    scaled = jnp.pad(scaled, ((0, 0), (0, PAD - width), (0, 0)))
    pieces = scaled.reshape(queries, PAD, 2, 128).transpose(0, 2, 1, 3).reshape(8, PAD, 128)
    blocks = column_blocks(kx.reshape(1), out_basis_t)
    vs = [blocks[0]] + [shift_x(blocks[d], d) for d in range(1, NX)]
    pieces = lax.all_to_all(pieces, "dp", 0, 0, axis_index_groups=ZG)
    rows = NY * 128
    mixed = jnp.concatenate([in_basis.reshape(NX, rows, 128), pieces.reshape(NX, 2 * PAD, 128)], axis=1)
    mixed = lax.all_to_all(mixed, "tensor", 0, 0, axis_index_groups=XG)
    u4 = mixed[:, :rows]
    tie = (vs[1][:1, :1] + vs[2][:1, :1] + vs[3][:1, :1]) * 0
    pieces = after(mixed[:, rows:].reshape(NX, 2, PAD, 128), tie)
    tiles = lax.all_gather(pieces, "dp").reshape(NZ, 2, NX, 2, PAD, 128)

    a_part = jnp.einsum("xyed,yte->xdt", u4.reshape(NX, NY, 128, 128), x8, preferred_element_type=f32).astype(bf)
    a_parts = lax.all_to_all(a_part, "tensor", 0, 0, axis_index_groups=XG)

    y8 = y8.transpose(0, 2, 1, 3).reshape(NY * PAD, tokens)
    g_parts = [jnp.dot(v, y8, preferred_element_type=f32).astype(bf) for v in vs]
    tie = (g_parts[0][:1, :1] + g_parts[1][:1, :1] + g_parts[2][:1, :1] + g_parts[3][:1, :1]) * 0
    g_parts = [g_parts[0]] + [shift_x(g_parts[d], -d) for d in range(1, NX)]

    at = after(add_parts(a_parts).astype(bf), tie)
    at = jnp.broadcast_to(at, (NY, 128, tokens))
    at = lax.all_to_all(at, "tensor", 0, 0, axis_index_groups=YG)

    position = lax.broadcasted_iota(jnp.int32, (seqs, seq_len), 1)
    keep = (position < lengths[:, None]).astype(f32).reshape(1, tokens)
    g = (add_parts(g_parts) * keep).astype(bf)
    g = jnp.pad(g, ((0, PAD - width), (0, 0)))
    gs = [g] + [shift_x(g, d) for d in range(1, NX)]

    tile = score_tiles(kx.reshape(1), gs, at.reshape(NY * 128, tokens), tiles)
    totals = lax.all_to_all(tile, "tensor", 0, 0, tiled=True).sum(0)[: seqs * queries]
    norm_factor = (in_basis.shape[0] * out_basis_t.shape[1] * seq_len) ** (-0.5)
    return totals.reshape(seqs, queries) * norm_factor


def solution(mesh):
    placed = (
        P("dp", "tensor"),
        P("tensor", "dp"),
        P(None, "tensor"),
        P("tensor", None),
        P(None, "tensor", "dp"),
        P("tensor", "dp"),
        P(),
        P("dp"),
    )
    return jax.shard_map(
        local, mesh=mesh, in_specs=placed, out_specs=P("dp", None), check_vma=False
    )
```

```python
import jax
import jax.numpy as jnp
from jax import lax
from jax.experimental import pallas as pl
from jax.experimental.pallas import tpu as pltpu
from jax.sharding import PartitionSpec as P

NX, NY, NZ = 4, 8, 8
XG = [[x * NY + y for x in range(NX)] for y in range(NY)]
YG = [[x * NY + y for y in range(NY)] for x in range(NX)]
ZG = [[z * 2 + c for z in range(NZ)] for c in range(2)]
SEQ = 128
PAD = 176


def shift_x(array, by):
    perm = [(x * NY + y, (x + by) % NX * NY + y) for x in range(NX) for y in range(NY)]
    return lax.ppermute(array, "tensor", perm)


def pack_kernel(x_ref, y_ref, o_ref):
    tokens = x_ref.shape[0]
    width = y_ref.shape[0]
    o_ref[:tokens] = x_ref[...]
    for s in range(y_ref.shape[1] // SEQ):
        block = y_ref[:, s * SEQ : (s + 1) * SEQ]
        first = tokens + s * PAD
        o_ref[first : first + PAD] = jnp.concatenate([block, jnp.zeros((PAD - width, SEQ), block.dtype)], axis=0)


def packed(x, y):
    vmem = pl.BlockSpec(memory_space=pltpu.VMEM)
    return pl.pallas_call(
        pack_kernel,
        out_shape=jax.ShapeDtypeStruct((x.shape[0] + y.shape[1] // SEQ * PAD, SEQ), x.dtype),
        in_specs=[vmem] * 2,
        out_specs=vmem,
        cost_estimate=pl.CostEstimate(flops=0, bytes_accessed=1_000_000, transcendentals=0),
    )(x, y)


HALF = 96


def columns_kernel(where_ref, v_ref, o0_ref, o1_ref, o2_ref, o3_ref, all_ref):
    rows, columns = v_ref.shape
    width = columns // (NX * NY)
    for x in range(NX):
        for y in range(NY):
            first = (x * NY + y) * width
            if first + PAD <= columns:
                block = v_ref[:, first : first + PAD]
            else:
                block = jnp.concatenate(
                    [v_ref[:, first:], jnp.zeros((rows, first + PAD - columns), v_ref.dtype)], axis=1
                )
            block = jnp.concatenate([block, jnp.zeros((PAD - rows, PAD), v_ref.dtype)], axis=0)
            all_ref[x, :, y * PAD : (y + 1) * PAD] = block
    kx = where_ref[0]
    first = pl.multiple_of(where_ref[1] * (PAD - HALF), 16)
    o0_ref[...] = all_ref[kx]
    for d, o_ref in enumerate((o1_ref, o2_ref, o3_ref)):
        o_ref[...] = all_ref[(kx + d + 1) & (NX - 1), pl.ds(first, HALF), :]


def column_blocks(where, v):
    deep = NY * PAD
    vmem = pl.BlockSpec(memory_space=pltpu.VMEM)
    return pl.pallas_call(
        columns_kernel,
        out_shape=[jax.ShapeDtypeStruct((rows, deep), v.dtype) for rows in (PAD, HALF, HALF, HALF)],
        in_specs=[pl.BlockSpec(memory_space=pltpu.SMEM), vmem],
        out_specs=[vmem] * NX,
        scratch_shapes=[pltpu.VMEM((NX, PAD, deep), v.dtype)],
        compiler_params=pltpu.CompilerParams(vmem_limit_bytes=24 * 1024 * 1024),
        cost_estimate=pl.CostEstimate(flops=0, bytes_accessed=4_000_000, transcendentals=0),
    )(where, v)


def score_kernel(kx_ref, g0_ref, g1_ref, g2_ref, g3_ref, a_ref, s_ref, o_ref, lhs_ref):
    q = pl.program_id(0)
    queries = pl.num_programs(0)
    tokens = g0_ref.shape[1]
    for d in range(NX):
        fx = (kx_ref[0] - d) & (NX - 1)
        for y in range(NY):
            lhs_ref[d * PAD : (d + 1) * PAD, y * 128 : (y + 1) * 128] = s_ref[y % 2, y // 2 % 2, fx, y // 4]
    t = jnp.dot(lhs_ref[...], a_ref[...], preferred_element_type=jnp.float32)
    acc = jnp.zeros((8, tokens), jnp.float32)
    for d, g_ref in enumerate((g0_ref, g1_ref, g2_ref, g3_ref)):
        part = t[d * PAD : (d + 1) * PAD] * g_ref[...].astype(jnp.float32)
        acc += part.reshape(PAD // 8, 8, tokens).sum(0)
    per_token = jnp.sum(acc, axis=0, keepdims=True)
    lane = lax.broadcasted_iota(jnp.int32, o_ref.shape, 1)

    @pl.when(q == 0)
    def _():
        o_ref[...] = jnp.zeros_like(o_ref)

    out = o_ref[...]
    for s in range(tokens // SEQ):
        value = jnp.sum(per_token[:, s * SEQ : (s + 1) * SEQ], axis=1, keepdims=True)
        out = jnp.where(lane == s * queries + q, value, out)
    o_ref[...] = out


def score_tiles(kx, gs, at, tiles):
    tokens = at.shape[1]
    queries = tiles.shape[0] // 2
    whole = lambda q: (0, 0)
    return pl.pallas_call(
        score_kernel,
        grid=(queries,),
        out_shape=jax.ShapeDtypeStruct((NX * NY, 128), jnp.float32),
        in_specs=[pl.BlockSpec(memory_space=pltpu.SMEM)]
        + [pl.BlockSpec((PAD, tokens), whole)] * NX
        + [pl.BlockSpec(at.shape, whole), pl.BlockSpec((2,) + tiles.shape[1:], lambda q: (q, 0, 0, 0, 0, 0))],
        out_specs=pl.BlockSpec((NX * NY, 128), whole),
        scratch_shapes=[pltpu.VMEM((NX * PAD, NY * 128), jnp.bfloat16)],
        compiler_params=pltpu.CompilerParams(vmem_limit_bytes=48 * 1024 * 1024),
        cost_estimate=pl.CostEstimate(
            flops=2 * NX * queries * PAD * NY * 128 * tokens, bytes_accessed=9_000_000, transcendentals=0
        ),
    )(kx, *gs, at, tiles)


def add_parts(parts):
    wide = [parts[n].astype(jnp.float32) for n in range(NX)]
    return (wide[0] + wide[1]) + (wide[2] + wide[3])


def after(array, zero):
    first = (0,) * array.ndim
    corner = lax.slice(array, first, (1,) * array.ndim)
    return lax.dynamic_update_slice(array, corner + zero.reshape(corner.shape), first)


def both_halves(mine, core):
    other = lax.ppermute(mine, "dp", [(n, n ^ 1) for n in range(2 * NZ)])
    return jnp.where(core == 0, mine, other), jnp.where(core == 0, other, mine)


def local(activations, out_grads_t, in_basis, out_basis_t, query_proj, eigvals, damping, lengths):
    bf, f32 = jnp.bfloat16, jnp.float32
    tokens, width = activations.shape[0], out_grads_t.shape[0]
    seqs, queries = lengths.shape[0], query_proj.shape[0]
    seq_len = tokens // seqs
    kx = lax.shift_right_logical(lax.axis_index("tensor"), 3)
    core = lax.axis_index("dp") & 1

    both = packed(activations, out_grads_t)
    both = lax.all_gather(both, "tensor", axis_index_groups=YG)
    x8 = both[:, :tokens]
    y8 = both[:, tokens:].reshape(NY, seqs, PAD, seq_len)

    scaled = (query_proj.astype(f32) / (eigvals + damping[0])).astype(bf)
    scaled = jnp.pad(scaled, ((0, 0), (0, PAD - width), (0, 0)))
    pieces = scaled.reshape(queries, PAD, 2, 128).transpose(0, 2, 1, 3).reshape(8, PAD, 128)
    blocks = column_blocks(jnp.stack([kx, core]), out_basis_t)
    near = [shift_x(blocks[d], d) for d in range(1, NX)]
    tie = (near[0][:1, :1] + near[1][:1, :1] + near[2][:1, :1]) * 0
    pieces = lax.all_to_all(pieces, "dp", 0, 0, axis_index_groups=ZG)
    rows = NY * 128 // 2
    mine = lax.dynamic_index_in_dim(in_basis.reshape(NX, 2, rows, 128), core, 1, keepdims=False)
    mixed = jnp.concatenate([mine, pieces.reshape(NX, 2 * PAD, 128)], axis=1)
    mixed = lax.all_to_all(after(mixed, tie), "tensor", 0, 0, axis_index_groups=XG)
    u4 = jnp.stack(both_halves(mixed[:, :rows], core), axis=1)
    pieces = mixed[:, rows:].reshape(NX, 2, PAD, 128)
    tiles = lax.all_gather(pieces, "dp").reshape(NZ, 2, NX, 2, PAD, 128)

    a_part = jnp.einsum("xyed,yte->xdt", u4.reshape(NX, NY, 128, 128), x8, preferred_element_type=f32).astype(bf)
    a_parts = lax.all_to_all(a_part, "tensor", 0, 0, axis_index_groups=XG)

    near = after(jnp.stack(near), a_part[0, :1, :1] * 0)
    v_low, v_high = both_halves(near, core)
    vs = [blocks[0]] + [jnp.concatenate([v_low[n], v_high[n, 2 * HALF - PAD :]]) for n in range(NX - 1)]
    y8 = y8.transpose(0, 2, 1, 3).reshape(NY * PAD, tokens)
    g_parts = [jnp.dot(v, y8, preferred_element_type=f32).astype(bf) for v in vs]
    g_parts = [g_parts[0]] + [shift_x(g_parts[d], -d) for d in range(1, NX)]

    at = after(add_parts(a_parts).astype(bf), v_low[0, :1, :1] * 0)
    at = jnp.broadcast_to(at, (NY, 128, tokens))
    at = lax.all_to_all(at, "tensor", 0, 0, axis_index_groups=YG)

    position = lax.broadcasted_iota(jnp.int32, (seqs, seq_len), 1)
    keep = (position < lengths[:, None]).astype(f32).reshape(1, tokens)
    g = (add_parts(g_parts) * keep).astype(bf)
    gs = [g] + [shift_x(g, d) for d in range(1, NX)]

    tile = score_tiles(kx.reshape(1), gs, at.reshape(NY * 128, tokens), tiles)
    totals = lax.all_to_all(tile, "tensor", 0, 0, tiled=True).sum(0)[: seqs * queries]
    norm_factor = (in_basis.shape[0] * out_basis_t.shape[1] * seq_len) ** (-0.5)
    return totals.reshape(seqs, queries) * norm_factor


def solution(mesh):
    placed = (
        P("dp", "tensor"),
        P("tensor", "dp"),
        P(None, "tensor"),
        P("tensor", None),
        P(None, "tensor", "dp"),
        P("tensor", "dp"),
        P(),
        P("dp"),
    )
    return jax.shard_map(
        local, mesh=mesh, in_specs=placed, out_specs=P("dp", None), check_vma=False
    )
```

```python
import jax
import jax.numpy as jnp
from jax import lax
from jax.experimental import pallas as pl
from jax.experimental.pallas import tpu as pltpu
from jax.sharding import PartitionSpec as P

NX, NY, NZ = 4, 8, 8
XG = [[x * NY + y for x in range(NX)] for y in range(NY)]
YG = [[x * NY + y for y in range(NY)] for x in range(NX)]
ZG = [[z * 2 + c for z in range(NZ)] for c in range(2)]
SEQ = 128
PAD = 176


def shift_x(array, by):
    perm = [(x * NY + y, (x + by) % NX * NY + y) for x in range(NX) for y in range(NY)]
    return lax.ppermute(array, "tensor", perm)


def pack_kernel(x_ref, y_ref, o_ref):
    tokens = x_ref.shape[0]
    width = y_ref.shape[0]
    o_ref[:tokens] = x_ref[...]
    for s in range(y_ref.shape[1] // SEQ):
        block = y_ref[:, s * SEQ : (s + 1) * SEQ]
        first = tokens + s * PAD
        o_ref[first : first + PAD] = jnp.concatenate([block, jnp.zeros((PAD - width, SEQ), block.dtype)], axis=0)


def packed(x, y):
    vmem = pl.BlockSpec(memory_space=pltpu.VMEM)
    return pl.pallas_call(
        pack_kernel,
        out_shape=jax.ShapeDtypeStruct((x.shape[0] + y.shape[1] // SEQ * PAD, SEQ), x.dtype),
        in_specs=[vmem] * 2,
        out_specs=vmem,
        cost_estimate=pl.CostEstimate(flops=0, bytes_accessed=1_000_000, transcendentals=0),
    )(x, y)


HALF = 96


def columns_kernel(where_ref, v_ref, o0_ref, o1_ref, o2_ref, o3_ref, all_ref):
    rows, columns = v_ref.shape
    width = columns // (NX * NY)
    for x in range(NX):
        for y in range(NY):
            first = (x * NY + y) * width
            if first + PAD <= columns:
                block = v_ref[:, first : first + PAD]
            else:
                block = jnp.concatenate(
                    [v_ref[:, first:], jnp.zeros((rows, first + PAD - columns), v_ref.dtype)], axis=1
                )
            block = jnp.concatenate([block, jnp.zeros((PAD - rows, PAD), v_ref.dtype)], axis=0)
            all_ref[x, :, y * PAD : (y + 1) * PAD] = block
    kx = where_ref[0]
    first = pl.multiple_of(where_ref[1] * (PAD - HALF), 16)
    o0_ref[...] = all_ref[kx]
    for d, o_ref in enumerate((o1_ref, o2_ref, o3_ref)):
        o_ref[...] = all_ref[(kx + d + 1) & (NX - 1), pl.ds(first, HALF), :]


def column_blocks(where, v):
    deep = NY * PAD
    vmem = pl.BlockSpec(memory_space=pltpu.VMEM)
    return pl.pallas_call(
        columns_kernel,
        out_shape=[jax.ShapeDtypeStruct((rows, deep), v.dtype) for rows in (PAD, HALF, HALF, HALF)],
        in_specs=[pl.BlockSpec(memory_space=pltpu.SMEM), vmem],
        out_specs=[vmem] * NX,
        scratch_shapes=[pltpu.VMEM((NX, PAD, deep), v.dtype)],
        compiler_params=pltpu.CompilerParams(vmem_limit_bytes=24 * 1024 * 1024),
        cost_estimate=pl.CostEstimate(flops=0, bytes_accessed=4_000_000, transcendentals=0),
    )(where, v)


def score_kernel(kx_ref, g0_ref, g1_ref, g2_ref, g3_ref, a_ref, s_ref, o_ref, lhs_ref):
    q = pl.program_id(0)
    queries = pl.num_programs(0)
    tokens = g0_ref.shape[1]
    for d in range(NX):
        fx = (kx_ref[0] - d) & (NX - 1)
        for y in range(NY):
            lhs_ref[d * PAD : (d + 1) * PAD, y * 128 : (y + 1) * 128] = s_ref[y % 2, y // 2 % 2, fx, y // 4]
    t = jnp.dot(lhs_ref[...], a_ref[...], preferred_element_type=jnp.float32)
    acc = jnp.zeros((8, tokens), jnp.float32)
    for d, g_ref in enumerate((g0_ref, g1_ref, g2_ref, g3_ref)):
        part = t[d * PAD : (d + 1) * PAD] * g_ref[...].astype(jnp.float32)
        acc += part.reshape(PAD // 8, 8, tokens).sum(0)
    per_token = jnp.sum(acc, axis=0, keepdims=True)
    lane = lax.broadcasted_iota(jnp.int32, o_ref.shape, 1)

    @pl.when(q == 0)
    def _():
        o_ref[...] = jnp.zeros_like(o_ref)

    out = o_ref[...]
    for s in range(tokens // SEQ):
        value = jnp.sum(per_token[:, s * SEQ : (s + 1) * SEQ], axis=1, keepdims=True)
        out = jnp.where(lane == s * queries + q, value, out)
    o_ref[...] = out


def score_tiles(kx, gs, at, tiles):
    tokens = at.shape[1]
    queries = tiles.shape[0] // 2
    whole = lambda q: (0, 0)
    return pl.pallas_call(
        score_kernel,
        grid=(queries,),
        out_shape=jax.ShapeDtypeStruct((NX * NY, 128), jnp.float32),
        in_specs=[pl.BlockSpec(memory_space=pltpu.SMEM)]
        + [pl.BlockSpec((PAD, tokens), whole)] * NX
        + [pl.BlockSpec(at.shape, whole), pl.BlockSpec((2,) + tiles.shape[1:], lambda q: (q, 0, 0, 0, 0, 0))],
        out_specs=pl.BlockSpec((NX * NY, 128), whole),
        scratch_shapes=[pltpu.VMEM((NX * PAD, NY * 128), jnp.bfloat16)],
        compiler_params=pltpu.CompilerParams(vmem_limit_bytes=48 * 1024 * 1024),
        cost_estimate=pl.CostEstimate(
            flops=2 * NX * queries * PAD * NY * 128 * tokens, bytes_accessed=9_000_000, transcendentals=0
        ),
    )(kx, *gs, at, tiles)


def add_parts(parts):
    wide = [parts[n].astype(jnp.float32) for n in range(NX)]
    return (wide[0] + wide[1]) + (wide[2] + wide[3])


def after(array, zero):
    first = (0,) * array.ndim
    corner = lax.slice(array, first, (1,) * array.ndim)
    return lax.dynamic_update_slice(array, corner + zero.reshape(corner.shape), first)


def both_halves(mine, core):
    other = lax.ppermute(mine, "dp", [(n, n ^ 1) for n in range(2 * NZ)])
    return jnp.where(core == 0, mine, other), jnp.where(core == 0, other, mine)


def local(activations, out_grads_t, in_basis, out_basis_t, query_proj, eigvals, damping, lengths):
    bf, f32 = jnp.bfloat16, jnp.float32
    tokens, width = activations.shape[0], out_grads_t.shape[0]
    seqs, queries = lengths.shape[0], query_proj.shape[0]
    seq_len = tokens // seqs
    kx = lax.shift_right_logical(lax.axis_index("tensor"), 3)
    core = lax.axis_index("dp") & 1

    both = packed(activations, out_grads_t)
    both = lax.all_gather(both, "tensor", axis_index_groups=YG)
    x8 = both[:, :tokens]
    y8 = both[:, tokens:].reshape(NY, seqs, PAD, seq_len)

    scaled = (query_proj.astype(f32) / (eigvals + damping[0])).astype(bf)
    scaled = jnp.pad(scaled, ((0, 0), (0, PAD - width), (0, 0)))
    pieces = scaled.reshape(queries, PAD, 2, 128).transpose(0, 2, 1, 3).reshape(8, PAD, 128)
    blocks = column_blocks(jnp.stack([kx, core]), out_basis_t)
    near = [shift_x(blocks[d], d) for d in range(1, NX)]
    tie = (near[0][:1, :1] + near[1][:1, :1] + near[2][:1, :1]) * 0
    near = jnp.stack(near)
    v_low, v_high = both_halves(near, core)
    vs = [blocks[0]] + [jnp.concatenate([v_low[n], v_high[n, 2 * HALF - PAD :]]) for n in range(NX - 1)]

    pieces = lax.all_to_all(pieces, "dp", 0, 0, axis_index_groups=ZG)
    rows = NY * 128 // 2
    mine = lax.dynamic_index_in_dim(in_basis.reshape(NX, 2, rows, 128), core, 1, keepdims=False)
    mixed = jnp.concatenate([mine, pieces.reshape(NX, 2 * PAD, 128)], axis=1)
    mixed = lax.all_to_all(after(mixed, tie), "tensor", 0, 0, axis_index_groups=XG)
    u4 = jnp.stack(both_halves(mixed[:, :rows], core), axis=1)
    pieces = after(mixed[:, rows:].reshape(NX, 2, PAD, 128), v_low[0, :1, :1] * 0)
    tiles = lax.all_gather(pieces, "dp").reshape(NZ, 2, NX, 2, PAD, 128)

    a_part = jnp.einsum("xyed,yte->xdt", u4.reshape(NX, NY, 128, 128), x8, preferred_element_type=f32).astype(bf)
    a_parts = lax.all_to_all(a_part, "tensor", 0, 0, axis_index_groups=XG)

    y8 = y8.transpose(0, 2, 1, 3).reshape(NY * PAD, tokens)
    g_parts = [jnp.dot(v, y8, preferred_element_type=f32).astype(bf) for v in vs]
    g_parts = [g_parts[0]] + [shift_x(g_parts[d], -d) for d in range(1, NX)]

    at = jnp.broadcast_to(add_parts(a_parts).astype(bf), (NY, 128, tokens))
    at = lax.all_to_all(at, "tensor", 0, 0, axis_index_groups=YG)

    position = lax.broadcasted_iota(jnp.int32, (seqs, seq_len), 1)
    keep = (position < lengths[:, None]).astype(f32).reshape(1, tokens)
    g = (add_parts(g_parts) * keep).astype(bf)
    gs = [g] + [shift_x(g, d) for d in range(1, NX)]

    tile = score_tiles(kx.reshape(1), gs, at.reshape(NY * 128, tokens), tiles)
    totals = lax.all_to_all(tile, "tensor", 0, 0, tiled=True).sum(0)[: seqs * queries]
    norm_factor = (in_basis.shape[0] * out_basis_t.shape[1] * seq_len) ** (-0.5)
    return totals.reshape(seqs, queries) * norm_factor


def solution(mesh):
    placed = (
        P("dp", "tensor"),
        P("tensor", "dp"),
        P(None, "tensor"),
        P("tensor", None),
        P(None, "tensor", "dp"),
        P("tensor", "dp"),
        P(),
        P("dp"),
    )
    return jax.shard_map(
        local, mesh=mesh, in_specs=placed, out_specs=P("dp", None), check_vma=False
    )
```

```python
import jax
import jax.numpy as jnp
from jax import lax
from jax.experimental import pallas as pl
from jax.experimental.pallas import tpu as pltpu
from jax.sharding import PartitionSpec as P

NX, NY, NZ = 4, 8, 8
XG = [[x * NY + y for x in range(NX)] for y in range(NY)]
YG = [[x * NY + y for y in range(NY)] for x in range(NX)]
ZG = [[z * 2 + c for z in range(NZ)] for c in range(2)]
SEQ = 128
PAD = 176


def shift_x(array, by):
    perm = [(x * NY + y, (x + by) % NX * NY + y) for x in range(NX) for y in range(NY)]
    return lax.ppermute(array, "tensor", perm)


def pack_kernel(x_ref, y_ref, o_ref):
    tokens = x_ref.shape[0]
    width = y_ref.shape[0]
    o_ref[:tokens] = x_ref[...]
    for s in range(y_ref.shape[1] // SEQ):
        block = y_ref[:, s * SEQ : (s + 1) * SEQ]
        first = tokens + s * PAD
        o_ref[first : first + PAD] = jnp.concatenate([block, jnp.zeros((PAD - width, SEQ), block.dtype)], axis=0)


def packed(x, y):
    vmem = pl.BlockSpec(memory_space=pltpu.VMEM)
    return pl.pallas_call(
        pack_kernel,
        out_shape=jax.ShapeDtypeStruct((x.shape[0] + y.shape[1] // SEQ * PAD, SEQ), x.dtype),
        in_specs=[vmem] * 2,
        out_specs=vmem,
        cost_estimate=pl.CostEstimate(flops=0, bytes_accessed=1_000_000, transcendentals=0),
    )(x, y)


HALF = 96


def columns_kernel(where_ref, v_ref, o0_ref, o1_ref, o2_ref, o3_ref, all_ref):
    rows, columns = v_ref.shape
    width = columns // (NX * NY)
    for x in range(NX):
        for y in range(NY):
            first = (x * NY + y) * width
            if first + PAD <= columns:
                block = v_ref[:, first : first + PAD]
            else:
                block = jnp.concatenate(
                    [v_ref[:, first:], jnp.zeros((rows, first + PAD - columns), v_ref.dtype)], axis=1
                )
            block = jnp.concatenate([block, jnp.zeros((PAD - rows, PAD), v_ref.dtype)], axis=0)
            all_ref[x, :, y * PAD : (y + 1) * PAD] = block
    kx = where_ref[0]
    first = pl.multiple_of(where_ref[1] * (PAD - HALF), 16)
    o0_ref[...] = all_ref[kx]
    for d, o_ref in enumerate((o1_ref, o2_ref, o3_ref)):
        o_ref[...] = all_ref[(kx + d + 1) & (NX - 1), pl.ds(first, HALF), :]


def column_blocks(where, v):
    deep = NY * PAD
    vmem = pl.BlockSpec(memory_space=pltpu.VMEM)
    return pl.pallas_call(
        columns_kernel,
        out_shape=[jax.ShapeDtypeStruct((rows, deep), v.dtype) for rows in (PAD, HALF, HALF, HALF)],
        in_specs=[pl.BlockSpec(memory_space=pltpu.SMEM), vmem],
        out_specs=[vmem] * NX,
        scratch_shapes=[pltpu.VMEM((NX, PAD, deep), v.dtype)],
        compiler_params=pltpu.CompilerParams(vmem_limit_bytes=24 * 1024 * 1024),
        cost_estimate=pl.CostEstimate(flops=0, bytes_accessed=4_000_000, transcendentals=0),
    )(where, v)


def score_kernel(kx_ref, g0_ref, g1_ref, g2_ref, g3_ref, a_ref, s_ref, o_ref, lhs_ref):
    q = pl.program_id(0)
    queries = pl.num_programs(0)
    tokens = g0_ref.shape[1]
    for d in range(NX):
        fx = (kx_ref[0] - d) & (NX - 1)
        for y in range(NY):
            lhs_ref[d * PAD : (d + 1) * PAD, y * 128 : (y + 1) * 128] = s_ref[y % 2, y // 2 % 2, fx, y // 4]
    t = jnp.dot(lhs_ref[...], a_ref[...], preferred_element_type=jnp.float32)
    acc = jnp.zeros((8, tokens), jnp.float32)
    for d, g_ref in enumerate((g0_ref, g1_ref, g2_ref, g3_ref)):
        part = t[d * PAD : (d + 1) * PAD] * g_ref[...].astype(jnp.float32)
        acc += part.reshape(PAD // 8, 8, tokens).sum(0)
    per_token = jnp.sum(acc, axis=0, keepdims=True)
    lane = lax.broadcasted_iota(jnp.int32, o_ref.shape, 1)

    @pl.when(q == 0)
    def _():
        o_ref[...] = jnp.zeros_like(o_ref)

    out = o_ref[...]
    for s in range(tokens // SEQ):
        value = jnp.sum(per_token[:, s * SEQ : (s + 1) * SEQ], axis=1, keepdims=True)
        out = jnp.where(lane == s * queries + q, value, out)
    o_ref[...] = out


def score_tiles(kx, gs, at, tiles):
    tokens = at.shape[1]
    queries = tiles.shape[0] // 2
    whole = pl.BlockSpec(memory_space=pltpu.VMEM)
    return pl.pallas_call(
        score_kernel,
        grid=(queries,),
        out_shape=jax.ShapeDtypeStruct((NX * NY, 128), jnp.float32),
        in_specs=[pl.BlockSpec(memory_space=pltpu.SMEM)]
        + [whole] * (NX + 1)
        + [pl.BlockSpec((2,) + tiles.shape[1:], lambda q: (q, 0, 0, 0, 0, 0))],
        out_specs=whole,
        scratch_shapes=[pltpu.VMEM((NX * PAD, NY * 128), jnp.bfloat16)],
        compiler_params=pltpu.CompilerParams(vmem_limit_bytes=48 * 1024 * 1024),
        cost_estimate=pl.CostEstimate(
            flops=2 * NX * queries * PAD * NY * 128 * tokens, bytes_accessed=9_000_000, transcendentals=0
        ),
    )(kx, *gs, at, tiles)


def add_parts(parts):
    wide = [parts[n].astype(jnp.float32) for n in range(NX)]
    return (wide[0] + wide[1]) + (wide[2] + wide[3])


def after(array, zero):
    first = (0,) * array.ndim
    corner = lax.slice(array, first, (1,) * array.ndim)
    return lax.dynamic_update_slice(array, corner + zero.reshape(corner.shape), first)


def both_halves(mine, core):
    other = lax.ppermute(mine, "dp", [(n, n ^ 1) for n in range(2 * NZ)])
    return jnp.where(core == 0, mine, other), jnp.where(core == 0, other, mine)


def local(activations, out_grads_t, in_basis, out_basis_t, query_proj, eigvals, damping, lengths):
    bf, f32 = jnp.bfloat16, jnp.float32
    tokens, width = activations.shape[0], out_grads_t.shape[0]
    seqs, queries = lengths.shape[0], query_proj.shape[0]
    seq_len = tokens // seqs
    kx = lax.shift_right_logical(lax.axis_index("tensor"), 3)
    core = lax.axis_index("dp") & 1

    both = packed(activations, out_grads_t)
    both = lax.all_gather(both, "tensor", axis_index_groups=YG)
    x8 = both[:, :tokens]
    y8 = both[:, tokens:].reshape(NY, seqs, PAD, seq_len)

    scaled = (query_proj.astype(f32) / (eigvals + damping[0])).astype(bf)
    scaled = jnp.pad(scaled, ((0, 0), (0, PAD - width), (0, 0)))
    pieces = scaled.reshape(queries, PAD, 2, 128).transpose(0, 2, 1, 3).reshape(8, PAD, 128)
    blocks = column_blocks(jnp.stack([kx, core]), out_basis_t)
    near = [shift_x(blocks[d], d) for d in range(1, NX)]
    tie = (near[0][:1, :1] + near[1][:1, :1] + near[2][:1, :1]) * 0
    near = jnp.stack(near)
    v_low, v_high = both_halves(near, core)
    vs = [blocks[0]] + [jnp.concatenate([v_low[n], v_high[n, 2 * HALF - PAD :]]) for n in range(NX - 1)]

    pieces = lax.all_to_all(pieces, "dp", 0, 0, axis_index_groups=ZG)
    rows = NY * 128 // 2
    mine = lax.dynamic_index_in_dim(in_basis.reshape(NX, 2, rows, 128), core, 1, keepdims=False)
    mixed = jnp.concatenate([mine, pieces.reshape(NX, 2 * PAD, 128)], axis=1)
    mixed = lax.all_to_all(after(mixed, tie), "tensor", 0, 0, axis_index_groups=XG)
    u4 = jnp.stack(both_halves(mixed[:, :rows], core), axis=1)
    pieces = after(mixed[:, rows:].reshape(NX, 2, PAD, 128), v_low[0, :1, :1] * 0)
    tiles = lax.all_gather(pieces, "dp").reshape(NZ, 2, NX, 2, PAD, 128)

    a_part = jnp.einsum("xyed,yte->xdt", u4.reshape(NX, NY, 128, 128), x8, preferred_element_type=f32).astype(bf)
    a_parts = lax.all_to_all(a_part, "tensor", 0, 0, axis_index_groups=XG)

    y8 = after(y8.transpose(0, 2, 1, 3).reshape(NY * PAD, tokens), a_part[0, :1, :1] * 0)
    g_parts = [jnp.dot(v, y8, preferred_element_type=f32).astype(bf) for v in vs]
    g_parts = [g_parts[0]] + [shift_x(g_parts[d], -d) for d in range(1, NX)]

    at = jnp.broadcast_to(after(add_parts(a_parts).astype(bf), y8[:1, :1] * 0), (NY, 128, tokens))
    at = lax.all_to_all(at, "tensor", 0, 0, axis_index_groups=YG)

    position = lax.broadcasted_iota(jnp.int32, (seqs, seq_len), 1)
    keep = (position < lengths[:, None]).astype(f32).reshape(1, tokens)
    g = (add_parts(g_parts) * keep).astype(bf)
    gs = [g] + [shift_x(g, d) for d in range(1, NX)]

    tile = score_tiles(kx.reshape(1), gs, at.reshape(NY * 128, tokens), tiles)
    totals = lax.all_to_all(tile, "tensor", 0, 0, tiled=True).sum(0)[: seqs * queries]
    norm_factor = (in_basis.shape[0] * out_basis_t.shape[1] * seq_len) ** (-0.5)
    return totals.reshape(seqs, queries) * norm_factor


def solution(mesh):
    placed = (
        P("dp", "tensor"),
        P("tensor", "dp"),
        P(None, "tensor"),
        P("tensor", None),
        P(None, "tensor", "dp"),
        P("tensor", "dp"),
        P(),
        P("dp"),
    )
    return jax.shard_map(
        local, mesh=mesh, in_specs=placed, out_specs=P("dp", None), check_vma=False
    )
```

```python
import jax
import jax.numpy as jnp
from jax import lax
from jax.experimental import pallas as pl
from jax.experimental.pallas import tpu as pltpu
from jax.sharding import PartitionSpec as P

NX, NY, NZ = 4, 8, 8
XG = [[x * NY + y for x in range(NX)] for y in range(NY)]
YG = [[x * NY + y for y in range(NY)] for x in range(NX)]
ZG = [[z * 2 + c for z in range(NZ)] for c in range(2)]
SEQ = 128
PAD = 176


def shift_x(array, by):
    perm = [(x * NY + y, (x + by) % NX * NY + y) for x in range(NX) for y in range(NY)]
    return lax.ppermute(array, "tensor", perm)


def pack_kernel(x_ref, y_ref, o_ref):
    tokens = x_ref.shape[0]
    width = y_ref.shape[0]
    o_ref[:tokens] = x_ref[...]
    for s in range(y_ref.shape[1] // SEQ):
        block = y_ref[:, s * SEQ : (s + 1) * SEQ]
        first = tokens + s * PAD
        o_ref[first : first + PAD] = jnp.concatenate([block, jnp.zeros((PAD - width, SEQ), block.dtype)], axis=0)


def packed(x, y):
    vmem = pl.BlockSpec(memory_space=pltpu.VMEM)
    return pl.pallas_call(
        pack_kernel,
        out_shape=jax.ShapeDtypeStruct((x.shape[0] + y.shape[1] // SEQ * PAD, SEQ), x.dtype),
        in_specs=[vmem] * 2,
        out_specs=vmem,
        cost_estimate=pl.CostEstimate(flops=0, bytes_accessed=1_000_000, transcendentals=0),
    )(x, y)


HALF = 96


def columns_kernel(where_ref, v_ref, o0_ref, o1_ref, o2_ref, o3_ref, all_ref):
    rows, columns = v_ref.shape
    width = columns // (NX * NY)
    for x in range(NX):
        for y in range(NY):
            first = (x * NY + y) * width
            if first + PAD <= columns:
                block = v_ref[:, first : first + PAD]
            else:
                block = jnp.concatenate(
                    [v_ref[:, first:], jnp.zeros((rows, first + PAD - columns), v_ref.dtype)], axis=1
                )
            block = jnp.concatenate([block, jnp.zeros((PAD - rows, PAD), v_ref.dtype)], axis=0)
            all_ref[x, :, y * PAD : (y + 1) * PAD] = block
    kx = where_ref[0]
    first = pl.multiple_of(where_ref[1] * (PAD - HALF), 16)
    o0_ref[...] = all_ref[kx]
    for d, o_ref in enumerate((o1_ref, o2_ref, o3_ref)):
        o_ref[...] = all_ref[(kx + d + 1) & (NX - 1), pl.ds(first, HALF), :]


def column_blocks(where, v):
    deep = NY * PAD
    vmem = pl.BlockSpec(memory_space=pltpu.VMEM)
    return pl.pallas_call(
        columns_kernel,
        out_shape=[jax.ShapeDtypeStruct((rows, deep), v.dtype) for rows in (PAD, HALF, HALF, HALF)],
        in_specs=[pl.BlockSpec(memory_space=pltpu.SMEM), vmem],
        out_specs=[vmem] * NX,
        scratch_shapes=[pltpu.VMEM((NX, PAD, deep), v.dtype)],
        compiler_params=pltpu.CompilerParams(vmem_limit_bytes=24 * 1024 * 1024),
        cost_estimate=pl.CostEstimate(flops=0, bytes_accessed=4_000_000, transcendentals=0),
    )(where, v)


def join_kernel(where_ref, n1_ref, n2_ref, n3_ref, other_ref, o1_ref, o2_ref, o3_ref):
    skip = 2 * HALF - PAD
    for n, (n_ref, o_ref) in enumerate(((n1_ref, o1_ref), (n2_ref, o2_ref), (n3_ref, o3_ref))):

        @pl.when(where_ref[1] == 0)
        def _():
            o_ref[:HALF] = n_ref[...]
            o_ref[HALF:] = other_ref[n, skip:]

        @pl.when(where_ref[1] != 0)
        def _():
            o_ref[:HALF] = other_ref[n]
            o_ref[HALF:] = n_ref[skip:]


def joined(where, near, other):
    vmem = pl.BlockSpec(memory_space=pltpu.VMEM)
    return pl.pallas_call(
        join_kernel,
        out_shape=[jax.ShapeDtypeStruct((PAD, other.shape[2]), other.dtype)] * (NX - 1),
        in_specs=[pl.BlockSpec(memory_space=pltpu.SMEM)] + [vmem] * NX,
        out_specs=[vmem] * (NX - 1),
        compiler_params=pltpu.CompilerParams(vmem_limit_bytes=16 * 1024 * 1024),
        cost_estimate=pl.CostEstimate(flops=0, bytes_accessed=3_000_000, transcendentals=0),
    )(where, *near, other)


def score_kernel(kx_ref, g0_ref, g1_ref, g2_ref, g3_ref, a_ref, s_ref, o_ref, lhs_ref):
    q = pl.program_id(0)
    queries = pl.num_programs(0)
    tokens = g0_ref.shape[1]
    for d in range(NX):
        fx = (kx_ref[0] - d) & (NX - 1)
        for y in range(NY):
            lhs_ref[d * PAD : (d + 1) * PAD, y * 128 : (y + 1) * 128] = s_ref[y % 2, y // 2 % 2, fx, y // 4]
    t = jnp.dot(lhs_ref[...], a_ref[...], preferred_element_type=jnp.float32)
    acc = jnp.zeros((8, tokens), jnp.float32)
    for d, g_ref in enumerate((g0_ref, g1_ref, g2_ref, g3_ref)):
        part = t[d * PAD : (d + 1) * PAD] * g_ref[...].astype(jnp.float32)
        acc += part.reshape(PAD // 8, 8, tokens).sum(0)
    per_token = jnp.sum(acc, axis=0, keepdims=True)
    lane = lax.broadcasted_iota(jnp.int32, o_ref.shape, 1)

    @pl.when(q == 0)
    def _():
        o_ref[...] = jnp.zeros_like(o_ref)

    out = o_ref[...]
    for s in range(tokens // SEQ):
        value = jnp.sum(per_token[:, s * SEQ : (s + 1) * SEQ], axis=1, keepdims=True)
        out = jnp.where(lane == s * queries + q, value, out)
    o_ref[...] = out


def score_tiles(kx, gs, at, tiles):
    tokens = at.shape[1]
    queries = tiles.shape[0] // 2
    whole = lambda q: (0, 0)
    return pl.pallas_call(
        score_kernel,
        grid=(queries,),
        out_shape=jax.ShapeDtypeStruct((NX * NY, 128), jnp.float32),
        in_specs=[pl.BlockSpec(memory_space=pltpu.SMEM)]
        + [pl.BlockSpec((PAD, tokens), whole)] * NX
        + [pl.BlockSpec(at.shape, whole), pl.BlockSpec((2,) + tiles.shape[1:], lambda q: (q, 0, 0, 0, 0, 0))],
        out_specs=pl.BlockSpec((NX * NY, 128), whole),
        scratch_shapes=[pltpu.VMEM((NX * PAD, NY * 128), jnp.bfloat16)],
        compiler_params=pltpu.CompilerParams(vmem_limit_bytes=48 * 1024 * 1024),
        cost_estimate=pl.CostEstimate(
            flops=2 * NX * queries * PAD * NY * 128 * tokens, bytes_accessed=9_000_000, transcendentals=0
        ),
    )(kx, *gs, at, tiles)


def add_parts(parts):
    wide = [parts[n].astype(jnp.float32) for n in range(NX)]
    return (wide[0] + wide[1]) + (wide[2] + wide[3])


def after(array, zero):
    first = (0,) * array.ndim
    corner = lax.slice(array, first, (1,) * array.ndim)
    return lax.dynamic_update_slice(array, corner + zero.reshape(corner.shape), first)


def both_halves(mine, core):
    other = lax.ppermute(mine, "dp", [(n, n ^ 1) for n in range(2 * NZ)])
    return jnp.where(core == 0, mine, other), jnp.where(core == 0, other, mine)


def local(activations, out_grads_t, in_basis, out_basis_t, query_proj, eigvals, damping, lengths):
    bf, f32 = jnp.bfloat16, jnp.float32
    tokens, width = activations.shape[0], out_grads_t.shape[0]
    seqs, queries = lengths.shape[0], query_proj.shape[0]
    seq_len = tokens // seqs
    kx = lax.shift_right_logical(lax.axis_index("tensor"), 3)
    core = lax.axis_index("dp") & 1

    both = packed(activations, out_grads_t)
    both = lax.all_gather(both, "tensor", axis_index_groups=YG)
    x8 = both[:, :tokens]
    y8 = both[:, tokens:].reshape(NY, seqs, PAD, seq_len)

    scaled = (query_proj.astype(f32) / (eigvals + damping[0])).astype(bf)
    scaled = jnp.pad(scaled, ((0, 0), (0, PAD - width), (0, 0)))
    pieces = scaled.reshape(queries, PAD, 2, 128).transpose(0, 2, 1, 3).reshape(8, PAD, 128)
    where = jnp.stack([kx, core])
    blocks = column_blocks(where, out_basis_t)
    near = [shift_x(blocks[d], d) for d in range(1, NX)]
    tie = (near[0][:1, :1] + near[1][:1, :1] + near[2][:1, :1]) * 0
    other = lax.ppermute(jnp.stack(near), "dp", [(n, n ^ 1) for n in range(2 * NZ)])
    vs = [blocks[0]] + list(joined(where, near, other))

    pieces = lax.all_to_all(pieces, "dp", 0, 0, axis_index_groups=ZG)
    rows = NY * 128 // 2
    mine = lax.dynamic_index_in_dim(in_basis.reshape(NX, 2, rows, 128), core, 1, keepdims=False)
    mixed = jnp.concatenate([mine, pieces.reshape(NX, 2 * PAD, 128)], axis=1)
    mixed = lax.all_to_all(after(mixed, tie), "tensor", 0, 0, axis_index_groups=XG)
    u4 = jnp.stack(both_halves(mixed[:, :rows], core), axis=1)
    pieces = after(mixed[:, rows:].reshape(NX, 2, PAD, 128), vs[1][:1, :1] * 0)
    tiles = lax.all_gather(pieces, "dp").reshape(NZ, 2, NX, 2, PAD, 128)

    a_part = jnp.einsum("xyed,yte->xdt", u4.reshape(NX, NY, 128, 128), x8, preferred_element_type=f32).astype(bf)
    a_parts = lax.all_to_all(a_part, "tensor", 0, 0, axis_index_groups=XG)

    y8 = y8.transpose(0, 2, 1, 3).reshape(NY * PAD, tokens)
    g_parts = [jnp.dot(v, y8, preferred_element_type=f32).astype(bf) for v in vs]
    g_parts = [g_parts[0]] + [shift_x(g_parts[d], -d) for d in range(1, NX)]

    at = jnp.broadcast_to(add_parts(a_parts).astype(bf), (NY, 128, tokens))
    at = lax.all_to_all(at, "tensor", 0, 0, axis_index_groups=YG)

    position = lax.broadcasted_iota(jnp.int32, (seqs, seq_len), 1)
    keep = (position < lengths[:, None]).astype(f32).reshape(1, tokens)
    g = (add_parts(g_parts) * keep).astype(bf)
    gs = [g] + [shift_x(g, d) for d in range(1, NX)]

    tile = score_tiles(kx.reshape(1), gs, at.reshape(NY * 128, tokens), tiles)
    totals = lax.all_to_all(tile, "tensor", 0, 0, tiled=True).sum(0)[: seqs * queries]
    norm_factor = (in_basis.shape[0] * out_basis_t.shape[1] * seq_len) ** (-0.5)
    return totals.reshape(seqs, queries) * norm_factor


def solution(mesh):
    placed = (
        P("dp", "tensor"),
        P("tensor", "dp"),
        P(None, "tensor"),
        P("tensor", None),
        P(None, "tensor", "dp"),
        P("tensor", "dp"),
        P(),
        P("dp"),
    )
    return jax.shard_map(
        local, mesh=mesh, in_specs=placed, out_specs=P("dp", None), check_vma=False
    )
```

```python
import jax
import jax.numpy as jnp
from jax import lax
from jax.experimental import pallas as pl
from jax.experimental.pallas import tpu as pltpu
from jax.sharding import PartitionSpec as P

NX, NY, NZ = 4, 8, 8
XG = [[x * NY + y for x in range(NX)] for y in range(NY)]
YG = [[x * NY + y for y in range(NY)] for x in range(NX)]
ZG = [[z * 2 + c for z in range(NZ)] for c in range(2)]
SEQ = 128
PAD = 176


def shift_x(array, by):
    perm = [(x * NY + y, (x + by) % NX * NY + y) for x in range(NX) for y in range(NY)]
    return lax.ppermute(array, "tensor", perm)


def pack_kernel(x_ref, y_ref, o_ref):
    tokens = x_ref.shape[0]
    width = y_ref.shape[0]
    o_ref[:tokens] = x_ref[...]
    for s in range(y_ref.shape[1] // SEQ):
        block = y_ref[:, s * SEQ : (s + 1) * SEQ]
        first = tokens + s * PAD
        o_ref[first : first + PAD] = jnp.concatenate([block, jnp.zeros((PAD - width, SEQ), block.dtype)], axis=0)


def packed(x, y):
    vmem = pl.BlockSpec(memory_space=pltpu.VMEM)
    return pl.pallas_call(
        pack_kernel,
        out_shape=jax.ShapeDtypeStruct((x.shape[0] + y.shape[1] // SEQ * PAD, SEQ), x.dtype),
        in_specs=[vmem] * 2,
        out_specs=vmem,
        cost_estimate=pl.CostEstimate(flops=0, bytes_accessed=1_000_000, transcendentals=0),
    )(x, y)


HALF = 96


def columns_kernel(where_ref, v_ref, o0_ref, o1_ref, o2_ref, o3_ref, all_ref):
    rows, columns = v_ref.shape
    width = columns // (NX * NY)
    for x in range(NX):
        for y in range(NY):
            first = (x * NY + y) * width
            if first + PAD <= columns:
                block = v_ref[:, first : first + PAD]
            else:
                block = jnp.concatenate(
                    [v_ref[:, first:], jnp.zeros((rows, first + PAD - columns), v_ref.dtype)], axis=1
                )
            block = jnp.concatenate([block, jnp.zeros((PAD - rows, PAD), v_ref.dtype)], axis=0)
            all_ref[x, :, y * PAD : (y + 1) * PAD] = block
    kx = where_ref[0]
    first = pl.multiple_of(where_ref[1] * (PAD - HALF), 16)
    o0_ref[...] = all_ref[kx]
    for d, o_ref in enumerate((o1_ref, o2_ref, o3_ref)):
        o_ref[...] = all_ref[(kx + d + 1) & (NX - 1), pl.ds(first, HALF), :]


def column_blocks(where, v):
    deep = NY * PAD
    vmem = pl.BlockSpec(memory_space=pltpu.VMEM)
    return pl.pallas_call(
        columns_kernel,
        out_shape=[jax.ShapeDtypeStruct((rows, deep), v.dtype) for rows in (PAD, HALF, HALF, HALF)],
        in_specs=[pl.BlockSpec(memory_space=pltpu.SMEM), vmem],
        out_specs=[vmem] * NX,
        scratch_shapes=[pltpu.VMEM((NX, PAD, deep), v.dtype)],
        compiler_params=pltpu.CompilerParams(vmem_limit_bytes=24 * 1024 * 1024),
        cost_estimate=pl.CostEstimate(flops=0, bytes_accessed=4_000_000, transcendentals=0),
    )(where, v)


def score_kernel(kx_ref, g_ref, a_ref, s_ref, o_ref, lhs_ref):
    q = pl.program_id(0)
    queries = pl.num_programs(0)
    tokens = a_ref.shape[1]
    for d in range(NX):
        fx = (kx_ref[0] - d) & (NX - 1)
        for y in range(NY):
            lhs_ref[d * PAD : (d + 1) * PAD, y * 128 : (y + 1) * 128] = s_ref[y % 2, y // 2 % 2, fx, y // 4]
    t = jnp.dot(lhs_ref[...], a_ref[...], preferred_element_type=jnp.float32)
    acc = jnp.zeros((8, tokens), jnp.float32)
    for d in range(NX):
        part = t[d * PAD : (d + 1) * PAD] * g_ref[d].astype(jnp.float32)
        acc += part.reshape(PAD // 8, 8, tokens).sum(0)
    per_token = jnp.sum(acc, axis=0, keepdims=True)
    lane = lax.broadcasted_iota(jnp.int32, o_ref.shape, 1)

    @pl.when(q == 0)
    def _():
        o_ref[...] = jnp.zeros_like(o_ref)

    out = o_ref[...]
    for s in range(tokens // SEQ):
        value = jnp.sum(per_token[:, s * SEQ : (s + 1) * SEQ], axis=1, keepdims=True)
        out = jnp.where(lane == s * queries + q, value, out)
    o_ref[...] = out


def score_tiles(kx, g4, at, tiles):
    tokens = at.shape[1]
    queries = tiles.shape[0] // 2
    whole = lambda q: (0, 0)
    return pl.pallas_call(
        score_kernel,
        grid=(queries,),
        out_shape=jax.ShapeDtypeStruct((NX * NY, 128), jnp.float32),
        in_specs=[pl.BlockSpec(memory_space=pltpu.SMEM)]
        + [pl.BlockSpec((NX, PAD, tokens), lambda q: (0, 0, 0))]
        + [pl.BlockSpec(at.shape, whole), pl.BlockSpec((2,) + tiles.shape[1:], lambda q: (q, 0, 0, 0, 0, 0))],
        out_specs=pl.BlockSpec((NX * NY, 128), whole),
        scratch_shapes=[pltpu.VMEM((NX * PAD, NY * 128), jnp.bfloat16)],
        compiler_params=pltpu.CompilerParams(vmem_limit_bytes=48 * 1024 * 1024),
        cost_estimate=pl.CostEstimate(
            flops=2 * NX * queries * PAD * NY * 128 * tokens, bytes_accessed=9_000_000, transcendentals=0
        ),
    )(kx, g4, at, tiles)


def add_parts(parts):
    wide = [parts[n].astype(jnp.float32) for n in range(NX)]
    return (wide[0] + wide[1]) + (wide[2] + wide[3])


def after(array, zero):
    first = (0,) * array.ndim
    corner = lax.slice(array, first, (1,) * array.ndim)
    return lax.dynamic_update_slice(array, corner + zero.reshape(corner.shape), first)


def both_halves(mine, core):
    other = lax.ppermute(mine, "dp", [(n, n ^ 1) for n in range(2 * NZ)])
    return jnp.where(core == 0, mine, other), jnp.where(core == 0, other, mine)


def local(activations, out_grads_t, in_basis, out_basis_t, query_proj, eigvals, damping, lengths):
    bf, f32 = jnp.bfloat16, jnp.float32
    tokens, width = activations.shape[0], out_grads_t.shape[0]
    seqs, queries = lengths.shape[0], query_proj.shape[0]
    seq_len = tokens // seqs
    kx = lax.shift_right_logical(lax.axis_index("tensor"), 3)
    core = lax.axis_index("dp") & 1

    both = packed(activations, out_grads_t)
    both = lax.all_gather(both, "tensor", axis_index_groups=YG)
    x8 = both[:, :tokens]
    y8 = both[:, tokens:].reshape(NY, seqs, PAD, seq_len)

    scaled = (query_proj.astype(f32) / (eigvals + damping[0])).astype(bf)
    scaled = jnp.pad(scaled, ((0, 0), (0, PAD - width), (0, 0)))
    pieces = scaled.reshape(queries, PAD, 2, 128).transpose(0, 2, 1, 3).reshape(8, PAD, 128)
    blocks = column_blocks(jnp.stack([kx, core]), out_basis_t)
    near = [shift_x(blocks[d], d) for d in range(1, NX)]
    tie = (near[0][:1, :1] + near[1][:1, :1] + near[2][:1, :1]) * 0
    near = jnp.stack(near)
    v_low, v_high = both_halves(near, core)
    vs = [blocks[0]] + [jnp.concatenate([v_low[n], v_high[n, 2 * HALF - PAD :]]) for n in range(NX - 1)]

    pieces = lax.all_to_all(pieces, "dp", 0, 0, axis_index_groups=ZG)
    rows = NY * 128 // 2
    mine = lax.dynamic_index_in_dim(in_basis.reshape(NX, 2, rows, 128), core, 1, keepdims=False)
    mixed = jnp.concatenate([mine, pieces.reshape(NX, 2 * PAD, 128)], axis=1)
    mixed = lax.all_to_all(after(mixed, tie), "tensor", 0, 0, axis_index_groups=XG)
    u4 = jnp.stack(both_halves(mixed[:, :rows], core), axis=1)
    pieces = after(mixed[:, rows:].reshape(NX, 2, PAD, 128), v_low[0, :1, :1] * 0)
    tiles = lax.all_gather(pieces, "dp").reshape(NZ, 2, NX, 2, PAD, 128)

    a_part = jnp.einsum("xyed,yte->xdt", u4.reshape(NX, NY, 128, 128), x8, preferred_element_type=f32).astype(bf)
    a_parts = lax.all_to_all(a_part, "tensor", 0, 0, axis_index_groups=XG)

    y8 = y8.transpose(0, 2, 1, 3).reshape(NY * PAD, tokens)
    g_parts = [jnp.dot(v, y8, preferred_element_type=f32).astype(bf) for v in vs]
    g_parts = [g_parts[0]] + [shift_x(g_parts[d], -d) for d in range(1, NX)]

    at = jnp.broadcast_to(add_parts(a_parts).astype(bf), (NY, 128, tokens))
    at = lax.all_to_all(at, "tensor", 0, 0, axis_index_groups=YG)

    position = lax.broadcasted_iota(jnp.int32, (seqs, seq_len), 1)
    keep = (position < lengths[:, None]).astype(f32).reshape(1, tokens)
    g = (add_parts(g_parts) * keep).astype(bf)
    gs = [g] + [shift_x(g, d) for d in range(1, NX)]

    tile = score_tiles(kx.reshape(1), jnp.stack(gs), at.reshape(NY * 128, tokens), tiles)
    totals = lax.all_to_all(tile, "tensor", 0, 0, tiled=True).sum(0)[: seqs * queries]
    norm_factor = (in_basis.shape[0] * out_basis_t.shape[1] * seq_len) ** (-0.5)
    return totals.reshape(seqs, queries) * norm_factor


def solution(mesh):
    placed = (
        P("dp", "tensor"),
        P("tensor", "dp"),
        P(None, "tensor"),
        P("tensor", None),
        P(None, "tensor", "dp"),
        P("tensor", "dp"),
        P(),
        P("dp"),
    )
    return jax.shard_map(
        local, mesh=mesh, in_specs=placed, out_specs=P("dp", None), check_vma=False
    )
```
